32 devices in a mesh: bag: 8 (over z, core), ulysses: 4 (over y, x).
Axes of the slice: x: 2, y: 2, z: 4, core: 2. Of those that a mesh axis runs over, the one named last changes fastest.
Arguments:
- queries: bfloat16 [2048, 4096], P(('bag', 'ulysses')), may hold values from -13 to 13
- keys: bfloat16 [2048, 4096], P(('bag', 'ulysses')), may hold values from -13 to 13
- values: bfloat16 [2048, 4096], P(('bag', 'ulysses')), may hold values from -6 to 6
- span_route: int32 [8, 4, 8], P('bag'), may hold values from 0 to 7, each once within a row
- seq_lengths: int32 [8, 4], P('bag'), may hold values from 1 to 128, 256 in all within a row
Outputs:
- attended: bfloat16 [2048, 4096], P(('bag', 'ulysses'))
The draws below stay inside these ranges and needn't reach their ends.
Inputs may be any that keep to these rules, and one draw needn't show every extreme that they name: For each b and u, span_route[b, u, 0 to 7] is a permutation of the bags. `seq_lengths`: row B lists bag B's 4 sequence lengths in packed order; each row sums to 256 and its largest entry is 128.
All inputs are finite; a program needn't handle non-finite values.
Results may differ from the reference program's by a relative error of at most 0.0049.
Values may be sent and summed in bfloat16 or wider, within the bound.
No kernel may reach another device: no remote copies, remote signals or barrier semaphores. Data moves between devices by JAX's collectives and lax.ppermute only.
A program may use at most 64 MiB of HBM per device.

```python
import math
import jax
import jax.numpy as jnp
import numpy as np
from jax import lax

HEADS = 32
HDIM = 128
TOK_DEV = 64
SEQ_BAG = 4
TOKENS = 2048
BAG_TOK = 256
MAX_LEN = 128
N_BAG = 8
N_ULYSSES = 4


def draw_queries(key, part):
    return jnp.clip(jax.random.normal(jax.random.fold_in(key, 11), (TOKENS, HEADS * HDIM), jnp.float32), -6.0, 6.0).astype(jnp.bfloat16)


def draw_keys(key, part):
    return jnp.clip(jax.random.normal(jax.random.fold_in(key, 12), (TOKENS, HEADS * HDIM), jnp.float32), -6.0, 6.0).astype(jnp.bfloat16)


def levels(rng, dims, pieces, smallest, top_value):
    gain, own = 1.0, jax.random.fold_in(rng, 6)
    for dim, blocks in pieces:
        heights = jnp.exp(jax.random.uniform(jax.random.fold_in(own, dim), (blocks,), jnp.float32, smallest / len(pieces), top_value / len(pieces)))
        gain = gain * jnp.repeat(heights, dims[dim] // blocks).reshape([-1 if axis == dim else 1 for axis in range(len(dims))])
    return gain


def length_profile(count, total, most, skew):
    loads = [(1 << 20) // math.isqrt(standing ** skew) + 1 for standing in range(2, count + 1)]
    spare, counts = total - most - (count - 1), [1] * (count - 1)
    while spare > 0:
        movable = [i for i in range(count - 1) if counts[i] < most]
        pool, left = sum([loads[i] for i in movable]), spare
        for i in movable:
            more = min(most - counts[i], max(1, left * loads[i] // pool), spare)
            counts[i] = counts[i] + more
            spare = spare - more
    return np.array([most] + counts)


def uneven_parts(rng, amount, total, reach, skew):
    if amount == 2:
        one = jax.random.randint(rng, (), max(1, total - reach), min(reach, total - 1) + 1)
        return jnp.stack([one, total - one])
    tallies = jnp.asarray(length_profile(amount, total, reach, skew), jnp.int32)
    pairs = (amount - 1) // 2
    giver, receiver = tallies[1:1 + 2 * pairs:2], tallies[2:2 + 2 * pairs:2]
    margin = jnp.minimum(giver - 1, reach - receiver)
    moved = jax.random.randint(jax.random.fold_in(rng, 1), (pairs,), 0, 1 << 20) % (margin + 1)
    tallies = tallies.at[1:1 + 2 * pairs:2].set(giver - moved).at[2:2 + 2 * pairs:2].set(receiver + moved)
    return tallies[jax.random.permutation(jax.random.fold_in(rng, 2), amount)]


def noise(own_key, extent, width, reach, cuts=(), kind=jnp.bfloat16):
    entries = width * jax.random.normal(own_key, extent, jnp.float32)
    if cuts:
        entries = entries * levels(own_key, extent, cuts, -0.22, 0.18)
    return jnp.clip(entries, -reach, reach).astype(kind)


def setup_inputs(seed: int = 0) -> dict:
    key_of = jax.random.split(jax.random.key(seed), 6)
    return {
        "queries": draw_queries(jax.random.fold_in(key_of[5], 71), 0),
        "keys": draw_keys(jax.random.fold_in(key_of[5], 71), 0),
        "values": noise(key_of[2], (TOKENS, HEADS * HDIM), 1.0, 6.0, ((0, 32),)),
        "span_route": jax.vmap(lambda own: jax.random.permutation(own, N_BAG))(jax.random.split(key_of[3], N_BAG * N_ULYSSES)).reshape((N_BAG, N_ULYSSES, N_BAG)).astype(jnp.int32),
        "seq_lengths": jax.vmap(lambda own: uneven_parts(own, SEQ_BAG, BAG_TOK, MAX_LEN, 2))(jax.random.split(key_of[4], N_BAG)).reshape((N_BAG, SEQ_BAG)).astype(jnp.int32),
    }


def attend_bag(operands):
    query_bag, key_bag, value_bag, lengths = operands
    bag_tok = query_bag.shape[0]
    seq_ends = jnp.cumsum(lengths).astype(jnp.int32)
    positions = jnp.arange(bag_tok, dtype=jnp.int32)
    sequence = lax.optimization_barrier(jnp.sum((positions[:, None] >= seq_ends[None, :]).astype(jnp.int32), axis=1))
    same_seq = sequence[:, None] == sequence[None, :]
    query_f = query_bag.reshape(bag_tok, HEADS, HDIM).astype(jnp.float32)
    key_f = key_bag.reshape(bag_tok, HEADS, HDIM).astype(jnp.float32)
    value_f = value_bag.reshape(bag_tok, HEADS, HDIM).astype(jnp.float32)
    scores = jnp.einsum('qhd,khd->hqk', query_f, key_f) * (1.0 / math.sqrt(HDIM))
    scores = jnp.where(same_seq[None, :, :], scores, -jnp.inf)
    row_max = lax.optimization_barrier(jnp.max(scores, axis=-1, keepdims=True))
    expo = jnp.exp(scores - row_max)
    weights = (expo / lax.optimization_barrier(jnp.sum(expo, axis=-1, keepdims=True))).astype(jnp.bfloat16)
    output = jnp.einsum('hqk,khd->qhd', weights.astype(jnp.float32), value_f)
    return output.astype(jnp.bfloat16).reshape(bag_tok, HEADS * HDIM)

def reference(queries, keys, values, span_route, seq_lengths):
    span_len = TOK_DEV // N_BAG
    bag_tok = TOK_DEV * N_ULYSSES
    row_width = HEADS * HDIM
    inverse = jnp.argsort(span_route, axis=-1).astype(jnp.int32)
    dest_idx = jnp.arange(N_BAG, dtype=jnp.int32)[:, None, None, None]
    group_idx = jnp.arange(N_ULYSSES, dtype=jnp.int32)[None, :, None, None]
    source_idx = jnp.arange(N_BAG, dtype=jnp.int32)[None, None, :, None]
    offset_idx = jnp.arange(span_len, dtype=jnp.int32)[None, None, None, :]
    span_idx = inverse[source_idx, group_idx, dest_idx]
    token_idx = ((source_idx * N_ULYSSES + group_idx) * TOK_DEV + span_idx * span_len + offset_idx).astype(jnp.int32)
    token_idx = token_idx.reshape(N_BAG, bag_tok)
    packed_q = queries[token_idx]
    packed_k = keys[token_idx]
    packed_v = values[token_idx]
    packed_out = lax.map(attend_bag, (packed_q, packed_k, packed_v, seq_lengths))
    owner_bag = jnp.arange(N_BAG, dtype=jnp.int32)[:, None, None, None]
    owner_group = jnp.arange(N_ULYSSES, dtype=jnp.int32)[None, :, None, None]
    destination = span_route[:, :, :, None]
    flat_idx = (destination * bag_tok + (owner_group * N_BAG + owner_bag) * span_len + offset_idx).astype(jnp.int32)
    flat_idx = flat_idx.reshape(TOKENS)
    return packed_out.reshape(N_BAG * bag_tok, row_width)[flat_idx]
```

```python
import math

import jax
import jax.numpy as jnp
from jax import lax
from jax.experimental import pallas as pl
from jax.experimental.pallas import tpu as pltpu
from jax.sharding import PartitionSpec as P

HEADS = 32
HDIM = 128
PARTS = 1
ROW_TILE = 8
AXES = ("bag", "ulysses")


def pack_spans(route_mine, arrays, group_count, parts):
    bag_count, span_len, row_width = arrays[0].shape
    width = row_width // group_count // parts
    kinds = len(arrays)

    def kernel(route_ref, *refs):
        sources, targets, sems = refs[:kinds], refs[kinds : kinds + parts], refs[-1]
        for part in range(parts):

            def one_span(span, carry, part=part):
                bag = route_ref[span]
                for group in range(group_count):
                    first = (group * parts + part) * width
                    for kind in range(kinds):
                        pltpu.make_async_copy(
                            sources[kind].at[span, :, pl.ds(first, width)],
                            targets[part].at[bag * group_count + group, kind],
                            sems.at[part],
                        ).start()
                return carry

            lax.fori_loop(0, bag_count, one_span, 0, unroll=True)
        for part in range(parts):
            pltpu.make_async_copy(targets[part], targets[part], sems.at[part]).wait()

    shape = (bag_count * group_count, kinds, span_len, width)
    return pl.pallas_call(
        kernel,
        out_shape=[jax.ShapeDtypeStruct(shape, arrays[0].dtype)] * parts,
        in_specs=[pl.BlockSpec(memory_space=pltpu.SMEM)] + [pl.BlockSpec(memory_space=pl.ANY)] * kinds,
        out_specs=[pl.BlockSpec(memory_space=pltpu.VMEM)] * parts,
        scratch_shapes=[pltpu.SemaphoreType.DMA((parts,))],
        name="pack_spans",
    )(route_mine, *arrays)


def unpack_spans(route_mine, pieces, bag_count, group_count):
    parts = len(pieces)
    span_len, width = pieces[0].shape[1:]
    row_width = width * parts * group_count

    def kernel(route_ref, *refs):
        sources, target, sem = refs[:parts], refs[parts], refs[-1]

        def one_span(span, carry):
            bag = route_ref[span]
            for part in range(parts):
                for group in range(group_count):
                    first = (group * parts + part) * width
                    pltpu.make_async_copy(
                        sources[part].at[bag * group_count + group],
                        target.at[span, :, pl.ds(first, width)],
                        sem,
                    ).start()
            return carry

        lax.fori_loop(0, bag_count, one_span, 0, unroll=True)
        pltpu.make_async_copy(target, target, sem).wait()

    return pl.pallas_call(
        kernel,
        out_shape=jax.ShapeDtypeStruct((bag_count, span_len, row_width), pieces[0].dtype),
        in_specs=[pl.BlockSpec(memory_space=pltpu.SMEM)] + [pl.BlockSpec(memory_space=pltpu.VMEM)] * parts,
        out_specs=pl.BlockSpec(memory_space=pl.ANY),
        scratch_shapes=[pltpu.SemaphoreType.DMA],
        name="unpack_spans",
    )(route_mine, *pieces)


def attend(lengths, packed, bag_count, group_count):
    slots, _, span_len, width = packed.shape
    bag_tok = slots * span_len
    block = min(256, bag_tok)
    block_slots = block // span_len
    heads_here = width // HDIM
    seq_bag = lengths.shape[0]
    scale = 1.0 / math.sqrt(HDIM)

    def sequence_of(row, length_ref):
        slot, offset = row // span_len, row % span_len
        owner, group = slot // group_count, slot % group_count
        position = (group * bag_count + owner) * span_len + offset
        end = jnp.int32(0)
        sequence = jnp.zeros(row.shape, jnp.int32)
        for entry in range(seq_bag):
            end = end + length_ref[entry]
            sequence = sequence + (position >= end).astype(jnp.int32)
        return sequence

    def kernel(length_ref, packed_ref, out_ref):
        key_seq = sequence_of(lax.broadcasted_iota(jnp.int32, (1, bag_tok), 1), length_ref)

        def rows(kind, first, count, head):
            tile = packed_ref[pl.ds(first, count), kind, :, head * HDIM : (head + 1) * HDIM]
            return tile.astype(jnp.float32).reshape(count * span_len, HDIM).astype(jnp.bfloat16)

        for index in range(bag_tok // block):
            row = index * block + lax.broadcasted_iota(jnp.int32, (block, 1), 0)
            same = sequence_of(row, length_ref) == key_seq
            for head in range(heads_here):
                query = rows(0, index * block_slots, block_slots, head)
                key = rows(1, 0, slots, head)
                value = rows(2, 0, slots, head)
                scores = lax.dot_general(query, key, (((1,), (1,)), ((), ())), preferred_element_type=jnp.float32)
                scores = jnp.where(same, scores * scale, -jnp.inf)
                expo = jnp.exp(scores - jnp.max(scores, axis=-1, keepdims=True))
                weights = (expo / jnp.sum(expo, axis=-1, keepdims=True)).astype(jnp.bfloat16)
                output = jnp.dot(weights, value, preferred_element_type=jnp.float32)
                out_ref[pl.ds(index * block_slots, block_slots), :, head * HDIM : (head + 1) * HDIM] = output.reshape(
                    block_slots, span_len, HDIM
                ).astype(out_ref.dtype)

    return pl.pallas_call(
        kernel,
        out_shape=jax.ShapeDtypeStruct((slots, span_len, width), packed.dtype),
        in_specs=[pl.BlockSpec(memory_space=pltpu.SMEM), pl.BlockSpec(memory_space=pltpu.VMEM)],
        out_specs=pl.BlockSpec(memory_space=pltpu.VMEM),
        compiler_params=pltpu.CompilerParams(vmem_limit_bytes=32 << 20),
        cost_estimate=pl.CostEstimate(
            flops=4 * bag_tok * bag_tok * width, bytes_accessed=4 * bag_tok * width * 2, transcendentals=bag_tok * bag_tok * heads_here
        ),
        name="attend_bag",
    )(lengths, packed)


def exchange(rows):
    return lax.all_to_all(rows, AXES, split_axis=0, concat_axis=0, tiled=True)


def shards(queries, keys, values, span_route, seq_lengths):
    bag_count = lax.axis_size("bag")
    group_count = lax.axis_size("ulysses")
    tok_dev, row_width = queries.shape
    span_len = tok_dev // bag_count
    parts = PARTS
    width = row_width // group_count // parts
    route_mine = lax.dynamic_index_in_dim(span_route[0], lax.axis_index("ulysses"), 0, keepdims=False)
    arrays = [rows.reshape(bag_count, span_len, row_width) for rows in (queries, keys, values)]
    direct = span_len % ROW_TILE == 0
    if direct:
        packed = pack_spans(route_mine, arrays, group_count, parts)
    else:
        inverse = jnp.argsort(route_mine)
        stacked = jnp.stack(arrays)[:, inverse].reshape(3, bag_count, span_len, group_count, parts, width)
        stacked = stacked.transpose(4, 1, 3, 0, 2, 5).reshape(parts, bag_count * group_count, 3, span_len, width)
        packed = [stacked[part] for part in range(parts)]
    returned = []
    for part in range(parts):
        arrived = exchange(packed[part])
        returned.append(exchange(attend(seq_lengths[0], arrived, bag_count, group_count)))
    if direct:
        result = unpack_spans(route_mine, returned, bag_count, group_count)
    else:
        stacked = jnp.stack(returned).reshape(parts, bag_count, group_count, span_len, width)
        result = stacked.transpose(1, 3, 2, 0, 4)[route_mine]
    return result.reshape(tok_dev, row_width)


def solution(mesh):
    placed = (
        P(("bag", "ulysses"), None),
        P(("bag", "ulysses"), None),
        P(("bag", "ulysses"), None),
        P("bag", None, None),
        P("bag", None),
    )
    return jax.shard_map(
        shards, mesh=mesh, in_specs=placed, out_specs=P(("bag", "ulysses"), None), check_vma=False
    )
```

```python
import math

import jax
import jax.numpy as jnp
from jax import lax
from jax.experimental import pallas as pl
from jax.experimental.pallas import tpu as pltpu
from jax.sharding import PartitionSpec as P

HDIM = 128
ROW_TILE = 8
MARGIN = 1 << 20
AXES = ("bag", "ulysses")


def pack_spans(span_route, arrays):
    bag_count, group_count, heads_here, span_len, width = arrays[0].shape
    kinds = len(arrays)
    payload = sum(rows.nbytes for rows in arrays)

    def kernel(route_hbm, *refs):
        sources, target, stage, route_ref, sem = refs[:kinds], refs[kinds], refs[-3], refs[-2], refs[-1]
        group = lax.axis_index("ulysses")
        copies = [pltpu.make_async_copy(sources[k], stage.at[k], sem.at[k]) for k in range(kinds)]
        for copy in copies:
            copy.start()
        route_copy = pltpu.make_async_copy(route_hbm, route_ref, sem.at[kinds])
        route_copy.start()
        route_copy.wait()
        for kind in range(kinds):
            copies[kind].wait()
            for span in range(bag_count):
                target[route_ref[0, group, span], :, kind] = stage[kind, span]

    shape = (bag_count, group_count, kinds, heads_here, span_len, width)
    packed = pl.pallas_call(
        kernel,
        out_shape=pltpu.VMEM(shape, arrays[0].dtype),
        in_specs=[pl.BlockSpec(memory_space=pl.ANY)] * (1 + kinds),
        out_specs=pl.BlockSpec(memory_space=pltpu.VMEM),
        scratch_shapes=[pltpu.VMEM((kinds, *arrays[0].shape), arrays[0].dtype), pltpu.SMEM(span_route.shape, span_route.dtype), pltpu.SemaphoreType.DMA((kinds + 1,))],
        compiler_params=pltpu.CompilerParams(vmem_limit_bytes=2 * payload + MARGIN),
        name="pack_spans",
    )(*[pltpu.with_memory_space_constraint(rows, pltpu.HBM) for rows in (span_route, *arrays)])
    return packed.reshape(bag_count * group_count, *shape[2:])


def unpack_spans(span_route, returned):
    bag_count, group_count = returned.shape[:2]

    def kernel(route_ref, source, target, sem):
        group = lax.axis_index("ulysses")
        for span in range(bag_count):
            pltpu.make_async_copy(source.at[route_ref[0, group, span]], target.at[span], sem).start()
        pltpu.make_async_copy(target, target, sem).wait()

    return pl.pallas_call(
        kernel,
        out_shape=jax.ShapeDtypeStruct(returned.shape, returned.dtype),
        in_specs=[pl.BlockSpec(memory_space=pltpu.SMEM), pl.BlockSpec(memory_space=pltpu.VMEM)],
        out_specs=pl.BlockSpec(memory_space=pl.ANY),
        scratch_shapes=[pltpu.SemaphoreType.DMA],
        compiler_params=pltpu.CompilerParams(vmem_limit_bytes=returned.nbytes + MARGIN),
        name="unpack_spans",
    )(span_route, returned)


def attend(lengths, packed, bag_count, group_count):
    slots, _, heads_here, span_len, width = packed.shape
    bag_tok = slots * span_len
    block = min(256, bag_tok)
    block_slots = block // span_len
    seq_bag = lengths.shape[1]
    scale = 1.0 / math.sqrt(width)

    def sequence_of(row, length_ref):
        slot, offset = row // span_len, row % span_len
        owner, group = slot // group_count, slot % group_count
        position = (group * bag_count + owner) * span_len + offset
        end = jnp.int32(0)
        sequence = jnp.zeros(row.shape, jnp.int32)
        for entry in range(seq_bag):
            end = end + length_ref[0, entry]
            sequence = sequence + (position >= end).astype(jnp.int32)
        return sequence

    def kernel(length_ref, packed_ref, out_ref):
        key_seq = sequence_of(lax.broadcasted_iota(jnp.int32, (1, bag_tok), 1), length_ref)

        def rows(kind, first, count, head):
            tile = packed_ref[pl.ds(first, count), kind, head]
            return tile.astype(jnp.float32).reshape(count * span_len, width).astype(jnp.bfloat16)

        def one_block(index, carry):
            first = index * block_slots
            row = index * block + lax.broadcasted_iota(jnp.int32, (block, 1), 0)
            same = sequence_of(row, length_ref) == key_seq
            scores = [
                lax.dot_general(
                    rows(0, first, block_slots, head),
                    rows(1, 0, slots, head),
                    (((1,), (1,)), ((), ())),
                    preferred_element_type=jnp.float32,
                )
                for head in range(heads_here)
            ]
            weights = []
            for score in scores:
                score = jnp.where(same, score * scale, -jnp.inf)
                expo = jnp.exp(score - jnp.max(score, axis=-1, keepdims=True))
                weights.append((expo * (1.0 / jnp.sum(expo, axis=-1, keepdims=True))).astype(jnp.bfloat16))
            for head in range(heads_here):
                output = jnp.dot(weights[head], rows(2, 0, slots, head), preferred_element_type=jnp.float32)
                output = output.reshape(block_slots, span_len, width).astype(out_ref.dtype)
                out_ref[pl.ds(first, block_slots), head] = output
            return carry

        if bag_tok == block:
            one_block(0, 0)
        else:
            lax.fori_loop(0, bag_tok // block, one_block, 0)

    return pl.pallas_call(
        kernel,
        out_shape=jax.ShapeDtypeStruct((slots, heads_here, span_len, width), packed.dtype),
        in_specs=[pl.BlockSpec(memory_space=pltpu.SMEM), pl.BlockSpec(memory_space=pltpu.VMEM)],
        out_specs=pl.BlockSpec(memory_space=pltpu.VMEM),
        compiler_params=pltpu.CompilerParams(vmem_limit_bytes=32 << 20),
        name="attend_bag",
    )(lengths, packed)


def exchange(rows):
    return lax.all_to_all(rows, AXES, split_axis=0, concat_axis=0, tiled=True)


def shards(queries, keys, values, span_route, seq_lengths):
    bag_count = lax.axis_size("bag")
    group_count = lax.axis_size("ulysses")
    tok_dev, row_width = queries.shape
    span_len = tok_dev // bag_count
    heads_here = row_width // HDIM // group_count
    arrays = [
        rows.reshape(bag_count, span_len, group_count, heads_here, HDIM).transpose(0, 2, 3, 1, 4)
        for rows in (queries, keys, values)
    ]
    direct = span_len % ROW_TILE == 0
    if direct:
        packed = pack_spans(span_route, arrays)
    else:
        route_mine = lax.dynamic_index_in_dim(span_route[0], lax.axis_index("ulysses"), 0, keepdims=False)
        packed = jnp.stack(arrays, axis=2)[jnp.argsort(route_mine)]
        packed = packed.reshape(bag_count * group_count, *packed.shape[2:])
    attended = attend(seq_lengths, exchange(packed), bag_count, group_count)
    returned = exchange(attended).reshape(bag_count, group_count, *attended.shape[1:])
    result = unpack_spans(span_route, returned) if direct else returned[route_mine]
    return result.transpose(0, 3, 1, 2, 4).reshape(tok_dev, row_width)


def solution(mesh):
    placed = (
        P(("bag", "ulysses"), None),
        P(("bag", "ulysses"), None),
        P(("bag", "ulysses"), None),
        P("bag", None, None),
        P("bag", None),
    )
    return jax.shard_map(
        shards, mesh=mesh, in_specs=placed, out_specs=P(("bag", "ulysses"), None), check_vma=False
    )
```

```python
import math

import jax
import jax.numpy as jnp
from jax import lax
from jax.experimental import pallas as pl
from jax.experimental.pallas import tpu as pltpu
from jax.sharding import PartitionSpec as P

HDIM = 128
ROW_TILE = 8
MARGIN = 1 << 20
AXES = ("bag", "ulysses")


def pack_spans(span_route, arrays):
    bag_count, group_count, heads_here, span_len, width = arrays[0].shape
    kinds = len(arrays)
    payload = sum(rows.nbytes for rows in arrays)

    def kernel(route_hbm, *refs):
        sources, target, stage, route_ref, sem = refs[:kinds], refs[kinds], refs[-3], refs[-2], refs[-1]
        group = lax.axis_index("ulysses")
        copies = [pltpu.make_async_copy(sources[k], stage.at[k], sem.at[k]) for k in range(kinds)]
        route_copy = pltpu.make_async_copy(route_hbm, route_ref, sem.at[kinds])
        route_copy.start()
        for copy in copies:
            copy.start()
        route_copy.wait()
        for kind in range(kinds):
            copies[kind].wait()
            for span in range(bag_count):
                target[route_ref[0, group, span], :, kind] = stage[kind, span]

    shape = (bag_count, group_count, kinds, heads_here, span_len, width)
    packed = pl.pallas_call(
        kernel,
        out_shape=pltpu.VMEM(shape, arrays[0].dtype),
        in_specs=[pl.BlockSpec(memory_space=pl.ANY)] * (1 + kinds),
        out_specs=pl.BlockSpec(memory_space=pltpu.VMEM),
        scratch_shapes=[
            pltpu.VMEM((kinds, *arrays[0].shape), arrays[0].dtype),
            pltpu.SMEM(span_route.shape, span_route.dtype),
            pltpu.SemaphoreType.DMA((kinds + 1,)),
        ],
        compiler_params=pltpu.CompilerParams(vmem_limit_bytes=2 * payload + MARGIN),
        name="pack_spans",
    )(*[pltpu.with_memory_space_constraint(rows, pltpu.HBM) for rows in (span_route, *arrays)])
    return packed.reshape(bag_count * group_count, *shape[2:])


def unpack_spans(span_route, returned):
    bag_count, group_count = returned.shape[:2]

    def kernel(route_ref, source, target, sem):
        group = lax.axis_index("ulysses")
        for span in range(bag_count):
            pltpu.make_async_copy(source.at[route_ref[0, group, span]], target.at[span], sem).start()
        pltpu.make_async_copy(target, target, sem).wait()

    return pl.pallas_call(
        kernel,
        out_shape=jax.ShapeDtypeStruct(returned.shape, returned.dtype),
        in_specs=[pl.BlockSpec(memory_space=pltpu.VMEM)] * 2,
        out_specs=pl.BlockSpec(memory_space=pl.ANY),
        scratch_shapes=[pltpu.SemaphoreType.DMA],
        compiler_params=pltpu.CompilerParams(vmem_limit_bytes=returned.nbytes + MARGIN),
        name="unpack_spans",
    )(span_route, returned)


def attend(lengths, packed, bag_count, group_count):
    slots, _, heads_here, span_len, width = packed.shape
    bag_tok = slots * span_len
    block = min(256, bag_tok)
    block_slots = block // span_len
    seq_bag = lengths.shape[1]
    scale = 1.0 / math.sqrt(width)

    def sequence_of(row, length_ref):
        slot, offset = row // span_len, row % span_len
        owner, group = slot // group_count, slot % group_count
        position = (group * bag_count + owner) * span_len + offset
        end = jnp.zeros((1, 1), jnp.int32)
        sequence = jnp.zeros(row.shape, jnp.int32)
        for entry in range(seq_bag):
            end = end + length_ref[:, entry : entry + 1]
            sequence = sequence + (position >= end).astype(jnp.int32)
        return sequence

    def kernel(length_ref, packed_ref, out_ref):
        key_seq = sequence_of(lax.broadcasted_iota(jnp.int32, (1, bag_tok), 1), length_ref)

        def rows(kind, first, count, head):
            tile = packed_ref[pl.ds(first, count), kind, head]
            return tile.astype(jnp.float32).reshape(count * span_len, width).astype(jnp.bfloat16)

        def one_block(index, carry):
            first = index * block_slots
            row = index * block + lax.broadcasted_iota(jnp.int32, (block, 1), 0)
            same = sequence_of(row, length_ref) == key_seq
            scores = [
                lax.dot_general(
                    rows(0, first, block_slots, head),
                    rows(1, 0, slots, head),
                    (((1,), (1,)), ((), ())),
                    preferred_element_type=jnp.float32,
                )
                for head in range(heads_here)
            ]
            weights = []
            for score in scores:
                score = jnp.where(same, score * scale, -jnp.inf)
                expo = jnp.exp(score - jnp.max(score, axis=-1, keepdims=True))
                weights.append((expo * (1.0 / jnp.sum(expo, axis=-1, keepdims=True))).astype(jnp.bfloat16))
            for head in range(heads_here):
                output = jnp.dot(weights[head], rows(2, 0, slots, head), preferred_element_type=jnp.float32)
                output = output.reshape(block_slots, span_len, width).astype(out_ref.dtype)
                out_ref[pl.ds(first, block_slots), head] = output
            return carry

        if bag_tok == block:
            one_block(0, 0)
        else:
            lax.fori_loop(0, bag_tok // block, one_block, 0)

    return pl.pallas_call(
        kernel,
        out_shape=jax.ShapeDtypeStruct((slots, heads_here, span_len, width), packed.dtype),
        in_specs=[pl.BlockSpec(memory_space=pltpu.VMEM)] * 2,
        out_specs=pl.BlockSpec(memory_space=pltpu.VMEM),
        compiler_params=pltpu.CompilerParams(vmem_limit_bytes=32 << 20),
        name="attend_bag",
    )(lengths, packed)


def exchange(rows):
    return lax.all_to_all(rows, AXES, split_axis=0, concat_axis=0, tiled=True)


def shards(queries, keys, values, span_route, seq_lengths):
    bag_count = lax.axis_size("bag")
    group_count = lax.axis_size("ulysses")
    tok_dev, row_width = queries.shape
    span_len = tok_dev // bag_count
    heads_here = row_width // HDIM // group_count
    arrays = [
        rows.reshape(bag_count, span_len, group_count, heads_here, HDIM).transpose(0, 2, 3, 1, 4)
        for rows in (queries, keys, values)
    ]
    direct = span_len % ROW_TILE == 0
    if direct:
        packed = pack_spans(span_route, arrays)
    else:
        route_mine = lax.dynamic_index_in_dim(span_route[0], lax.axis_index("ulysses"), 0, keepdims=False)
        packed = jnp.stack(arrays, axis=2)[jnp.argsort(route_mine)]
        packed = packed.reshape(bag_count * group_count, *packed.shape[2:])
    attended = attend(seq_lengths, exchange(packed), bag_count, group_count)
    returned = exchange(attended).reshape(bag_count, group_count, *attended.shape[1:])
    result = unpack_spans(span_route, returned) if direct else returned[route_mine]
    return result.transpose(0, 3, 1, 2, 4).reshape(tok_dev, row_width)


def solution(mesh):
    placed = (
        P(("bag", "ulysses"), None),
        P(("bag", "ulysses"), None),
        P(("bag", "ulysses"), None),
        P("bag", None, None),
        P("bag", None),
    )
    return jax.shard_map(
        shards, mesh=mesh, in_specs=placed, out_specs=P(("bag", "ulysses"), None), check_vma=False
    )
```

```python
import math

import jax
import jax.numpy as jnp
from jax import lax
from jax.experimental import pallas as pl
from jax.experimental.pallas import tpu as pltpu
from jax.sharding import PartitionSpec as P

HDIM = 128
ROW_TILE = 8
MARGIN = 1 << 20
CORES = 2
AXES = ("bag", "ulysses")


def pack_spans(span_route, arrays):
    bag_count, group_count, heads_here, span_len, width = arrays[0].shape
    kinds = len(arrays)
    payload = sum(rows.nbytes for rows in arrays)

    def kernel(route_hbm, *refs):
        sources, target, stage, route_ref, sem = refs[:kinds], refs[kinds], refs[-3], refs[-2], refs[-1]
        group = lax.axis_index("ulysses")
        copies = [pltpu.make_async_copy(sources[k], stage.at[k], sem.at[k]) for k in range(kinds)]
        route_copy = pltpu.make_async_copy(route_hbm, route_ref, sem.at[kinds])
        route_copy.start()
        for copy in copies:
            copy.start()
        route_copy.wait()
        for kind in range(kinds):
            copies[kind].wait()
            for span in range(bag_count):
                to = route_ref[0, group, span]
                target[:, to % CORES, to // CORES, kind] = stage[kind, span]

    shape = (group_count, CORES, bag_count // CORES, kinds, heads_here, span_len, width)
    packed = pl.pallas_call(
        kernel,
        out_shape=pltpu.VMEM(shape, arrays[0].dtype),
        in_specs=[pl.BlockSpec(memory_space=pl.ANY)] * (1 + kinds),
        out_specs=pl.BlockSpec(memory_space=pltpu.VMEM),
        scratch_shapes=[
            pltpu.VMEM((kinds, *arrays[0].shape), arrays[0].dtype),
            pltpu.SMEM(span_route.shape, span_route.dtype),
            pltpu.SemaphoreType.DMA((kinds + 1,)),
        ],
        compiler_params=pltpu.CompilerParams(vmem_limit_bytes=2 * payload + MARGIN),
        name="pack_spans",
    )(*[pltpu.with_memory_space_constraint(rows, pltpu.HBM) for rows in (span_route, *arrays)])
    return packed.reshape(bag_count * group_count, *shape[3:])


def unpack_spans(span_route, returned):
    group_count, _, chips = returned.shape[:3]
    bag_count = chips * CORES

    def kernel(route_ref, source, target, sem):
        group = lax.axis_index("ulysses")
        for span in range(bag_count):
            bag = route_ref[0, group, span]
            pltpu.make_async_copy(source.at[:, bag % CORES, bag // CORES], target.at[span], sem).start()
        pltpu.make_async_copy(target, target, sem).wait()

    return pl.pallas_call(
        kernel,
        out_shape=jax.ShapeDtypeStruct((bag_count, group_count, *returned.shape[3:]), returned.dtype),
        in_specs=[pl.BlockSpec(memory_space=pltpu.VMEM)] * 2,
        out_specs=pl.BlockSpec(memory_space=pl.ANY),
        scratch_shapes=[pltpu.SemaphoreType.DMA],
        compiler_params=pltpu.CompilerParams(vmem_limit_bytes=returned.nbytes + MARGIN),
        name="unpack_spans",
    )(span_route, returned)


def attend(lengths, packed, bag_count, group_count):
    slots, _, heads_here, span_len, width = packed.shape
    bag_tok = slots * span_len
    block = min(256, bag_tok)
    block_slots = block // span_len
    seq_bag = lengths.shape[1]
    scale = 1.0 / math.sqrt(width)

    def sequence_of(row, length_ref):
        slot, offset = row // span_len, row % span_len
        group, owner = slot // bag_count, slot % (bag_count // CORES) * CORES + slot % bag_count // (bag_count // CORES)
        position = (group * bag_count + owner) * span_len + offset
        end = jnp.zeros((1, 1), jnp.int32)
        sequence = jnp.zeros(row.shape, jnp.int32)
        for entry in range(seq_bag):
            end = end + length_ref[:, entry : entry + 1]
            sequence = sequence + (position >= end).astype(jnp.int32)
        return sequence

    def kernel(length_ref, packed_ref, out_ref):
        key_seq = sequence_of(lax.broadcasted_iota(jnp.int32, (1, bag_tok), 1), length_ref)

        def rows(kind, first, count, head):
            tile = packed_ref[pl.ds(first, count), kind, head]
            return tile.astype(jnp.float32).reshape(count * span_len, width).astype(jnp.bfloat16)

        def one_block(index, carry):
            first = index * block_slots
            row = index * block + lax.broadcasted_iota(jnp.int32, (block, 1), 0)
            same = sequence_of(row, length_ref) == key_seq
            scores = [
                lax.dot_general(
                    rows(0, first, block_slots, head),
                    rows(1, 0, slots, head),
                    (((1,), (1,)), ((), ())),
                    preferred_element_type=jnp.float32,
                )
                for head in range(heads_here)
            ]
            weights = []
            for score in scores:
                score = jnp.where(same, score * scale, -jnp.inf)
                expo = jnp.exp(score - jnp.max(score, axis=-1, keepdims=True))
                weights.append((expo * (1.0 / jnp.sum(expo, axis=-1, keepdims=True))).astype(jnp.bfloat16))
            for head in range(heads_here):
                output = jnp.dot(weights[head], rows(2, 0, slots, head), preferred_element_type=jnp.float32)
                output = output.reshape(block_slots, span_len, width).astype(out_ref.dtype)
                out_ref[pl.ds(first, block_slots), head] = output
            return carry

        if bag_tok == block:
            one_block(0, 0)
        else:
            lax.fori_loop(0, bag_tok // block, one_block, 0)

    return pl.pallas_call(
        kernel,
        out_shape=jax.ShapeDtypeStruct((slots, heads_here, span_len, width), packed.dtype),
        in_specs=[pl.BlockSpec(memory_space=pltpu.VMEM)] * 2,
        out_specs=pl.BlockSpec(memory_space=pltpu.VMEM),
        compiler_params=pltpu.CompilerParams(vmem_limit_bytes=32 << 20),
        name="attend_bag",
    )(lengths, packed)


def exchange(rows):
    bag_count, group_count = lax.axis_size("bag"), lax.axis_size("ulysses")
    order = [
        bag * group_count + group
        for group in range(group_count)
        for core in range(CORES)
        for bag in range(core, bag_count, CORES)
    ]
    return lax.all_to_all(rows, AXES, split_axis=0, concat_axis=0, tiled=True, axis_index_groups=[order])


def shards(queries, keys, values, span_route, seq_lengths):
    bag_count = lax.axis_size("bag")
    group_count = lax.axis_size("ulysses")
    tok_dev, row_width = queries.shape
    span_len = tok_dev // bag_count
    heads_here = row_width // HDIM // group_count
    arrays = [
        rows.reshape(bag_count, span_len, group_count, heads_here, HDIM).transpose(0, 2, 3, 1, 4)
        for rows in (queries, keys, values)
    ]
    slots = (group_count, CORES, bag_count // CORES)
    direct = span_len % ROW_TILE == 0
    if direct:
        packed = pack_spans(span_route, arrays)
    else:
        route_mine = lax.dynamic_index_in_dim(span_route[0], lax.axis_index("ulysses"), 0, keepdims=False)
        packed = jnp.stack(arrays, axis=2)[jnp.argsort(route_mine)]
        packed = packed.reshape(*slots[:0:-1], *packed.shape[1:]).swapaxes(0, 2)
        packed = packed.reshape(bag_count * group_count, *packed.shape[3:])
    attended = attend(seq_lengths, exchange(packed), bag_count, group_count)
    returned = exchange(attended).reshape(*slots, *attended.shape[1:])
    if direct:
        result = unpack_spans(span_route, returned)
    else:
        result = returned.swapaxes(0, 2).reshape(bag_count, group_count, *attended.shape[1:])[route_mine]
    return result.transpose(0, 3, 1, 2, 4).reshape(tok_dev, row_width)


def solution(mesh):
    placed = (
        P(("bag", "ulysses"), None),
        P(("bag", "ulysses"), None),
        P(("bag", "ulysses"), None),
        P("bag", None, None),
        P("bag", None),
    )
    return jax.shard_map(
        shards, mesh=mesh, in_specs=placed, out_specs=P(("bag", "ulysses"), None), check_vma=False
    )
```

```python
import math

import jax
import jax.numpy as jnp
from jax import lax
from jax.experimental import pallas as pl
from jax.experimental.pallas import tpu as pltpu
from jax.sharding import PartitionSpec as P

HDIM = 128
ROW_TILE = 8
MARGIN = 1 << 20
SPREAD = 1
BASE = 128
CORES = 2
AXES = ("bag", "ulysses")


def pack_spans(span_route, seq_lengths, arrays, direct_heads):
    bag_count, group_count, heads_here, span_len, width = arrays[0].shape
    kinds, chips = len(arrays), bag_count // CORES
    spread = heads_here - direct_heads
    payload = sum(rows.nbytes for rows in arrays)

    seq_bag = seq_lengths.shape[1]
    each = bag_count * group_count * spread

    def kernel(route_hbm, lengths_hbm, *refs):
        sources, (target, aside_q, aside_kv), (stage, lengths, route_ref, sem) = refs[:kinds], refs[kinds : kinds + 3], refs[-4:]
        group, bag = lax.axis_index("ulysses"), lax.axis_index("bag")
        copies = [pltpu.make_async_copy(sources[k], stage.at[k], sem.at[k]) for k in range(kinds)]
        route_copy = pltpu.make_async_copy(route_hbm, route_ref, sem.at[kinds])
        route_copy.start()
        for copy in copies:
            copy.start()
        lengths_copy = pltpu.make_async_copy(lengths_hbm, lengths, sem.at[kinds + 2])
        lengths_copy.start()
        route_copy.wait()
        lengths_copy.wait()
        row = lax.broadcasted_iota(jnp.int32, (span_len, width), 0)
        block = jnp.zeros((span_len, width), jnp.int32)
        for entry in range(seq_bag):
            length = lengths[:, entry : entry + 1]
            block = jnp.where(row == 2 * entry, length // BASE, jnp.where(row == 2 * entry + 1, length % BASE, block))
        aside_kv[(kinds - 1) * each] = block.astype(jnp.float32).astype(aside_kv.dtype)
        for kind in range(kinds):
            copies[kind].wait()
            for span in range(bag_count):
                to = route_ref[0, group, span]
                pltpu.make_async_copy(
                    stage.at[kind, span, :, pl.ds(0, direct_heads)],
                    target.at[:, to % CORES, to // CORES, kind],
                    sem.at[kinds + 1],
                ).start()
                for other in range(group_count):
                    block = ((other ^ group) * CORES + (to % CORES ^ bag % CORES)) * chips + to // CORES
                    block = block * spread
                    for head in range(spread):
                        rows = stage[kind, span, other, direct_heads + head]
                        if kind == 0:
                            aside_q[block + head] = rows
                        else:
                            aside_kv[(kind - 1) * each + block + head] = rows
        pltpu.make_async_copy(target, target, sem.at[kinds + 1]).wait()

    shape = (group_count, CORES, bag_count // CORES, kinds, direct_heads, span_len, width)
    shape_aside = [(each, span_len, width), ((kinds - 1) * each + 1, span_len, width)]
    dtype = arrays[0].dtype
    packed, aside_q, aside_kv = pl.pallas_call(
        kernel,
        out_shape=[jax.ShapeDtypeStruct(shape, dtype)] + [pltpu.VMEM(size, dtype) for size in shape_aside],
        in_specs=[pl.BlockSpec(memory_space=pl.ANY)] * (2 + kinds),
        out_specs=[pl.BlockSpec(memory_space=pl.ANY)] + [pl.BlockSpec(memory_space=pltpu.VMEM)] * 2,
        scratch_shapes=[
            pltpu.VMEM((kinds, *arrays[0].shape), dtype),
            pltpu.VMEM(seq_lengths.shape, seq_lengths.dtype),
            pltpu.SMEM(span_route.shape, span_route.dtype),
            pltpu.SemaphoreType.DMA((kinds + 3,)),
        ],
        compiler_params=pltpu.CompilerParams(vmem_limit_bytes=2 * payload + MARGIN),
        name="pack_spans",
    )(*[pltpu.with_memory_space_constraint(rows, pltpu.HBM) for rows in (span_route, seq_lengths, *arrays)])
    return packed.reshape(bag_count * group_count, *shape[3:]), aside_q, aside_kv


def unpack_spans(span_route, returned, pieces):
    group_count, _, chips, direct_heads, span_len, width = returned.shape
    bag_count = chips * CORES
    spread = pieces[0].shape[2]

    def kernel(route_ref, source, *refs):
        aside, (target, span_of, sem) = refs[:-3], refs[-3:]
        group, bag = lax.axis_index("ulysses"), lax.axis_index("bag")
        for span in range(bag_count):
            at = route_ref[0, group, span]
            span_of[at] = span
            pltpu.make_async_copy(
                source.at[:, at % CORES, at // CORES], target.at[span, :, pl.ds(0, direct_heads)], sem
            ).start()
        for distance, piece in enumerate(aside):
            for core in range(CORES):
                for chip in range(chips):
                    pltpu.make_async_copy(
                        piece.at[core, chip],
                        target.at[span_of[chip * CORES + (bag % CORES ^ core)], group ^ distance, pl.ds(direct_heads, spread)],
                        sem,
                    ).start()
        pltpu.make_async_copy(target, target, sem).wait()

    shape = (bag_count, group_count, direct_heads + spread, span_len, width)
    return pl.pallas_call(
        kernel,
        out_shape=jax.ShapeDtypeStruct(shape, returned.dtype),
        in_specs=[pl.BlockSpec(memory_space=pltpu.VMEM)] * (2 + len(pieces)),
        out_specs=pl.BlockSpec(memory_space=pl.ANY),
        scratch_shapes=[pltpu.SMEM((bag_count,), jnp.int32), pltpu.SemaphoreType.DMA],
        compiler_params=pltpu.CompilerParams(vmem_limit_bytes=2 * returned.nbytes + MARGIN),
        name="unpack_spans",
    )(span_route, returned, *pieces)


def swap(rows, axis, distance):
    return lax.ppermute(rows, axis, [(index, index ^ distance) for index in range(lax.axis_size(axis))])


def swap_cores(rows, axis):
    kept, sent = (lax.index_in_dim(rows, core, axis, keepdims=False) for core in range(CORES))
    return jnp.stack([kept, swap(sent, "bag", 1)], axis=axis)


def swap_groups(rows):
    return [rows[0]] + [swap(rows[distance], "ulysses", distance) for distance in range(1, rows.shape[0])]


def merge(queries, near, across):
    count, pair = queries.shape[0], near.shape[0] - 1
    size = queries.shape[1:]

    def kernel(query_ref, near_ref, across_ref, out_ref, length_ref):
        out_ref[:count] = query_ref[...]
        for index, ref in enumerate((near_ref, across_ref)):
            out_ref[count + index * pair : count + (index + 1) * pair] = ref[:pair]
            length_ref[index] = ref[pair]

    return pl.pallas_call(
        kernel,
        out_shape=[pltpu.VMEM((count + 2 * pair, *size), queries.dtype), pltpu.VMEM((2, *size), queries.dtype)],
        in_specs=[pl.BlockSpec(memory_space=pltpu.VMEM)] * 3,
        out_specs=[pl.BlockSpec(memory_space=pltpu.VMEM)] * 2,
        compiler_params=pltpu.CompilerParams(vmem_limit_bytes=4 << 20),
        cost_estimate=pl.CostEstimate(flops=1 << 35, bytes_accessed=1 << 26, transcendentals=0),
        name="merge",
    )(queries, near, across)


def gather_chips(near, lengths):
    chips = lax.axis_size("bag") // CORES
    size, distances = near.shape[1:], [0, chips // 2]
    step = chips // 4
    while step:
        count = near.shape[0]
        flat = jnp.concatenate([near.reshape(-1, *lengths.shape[1:]), lengths])
        flat = swap(flat, "bag", step * CORES)
        near = jnp.concatenate([near, flat[:-count].reshape(count, *size)])
        lengths = jnp.concatenate([lengths, flat[-count:]])
        distances, step = distances + [distance ^ step for distance in distances], step // 2
    order = [distances.index(distance) for distance in range(chips)]
    return jnp.stack([near[index] for index in order]), jnp.stack([lengths[index] for index in order])


def attend_plane(lengths, queries, keys_values, seq_bag, bag_count):
    group_count, _, chips, heads, span_len, width = queries.shape
    block = group_count * CORES * span_len
    scale = 1.0 / math.sqrt(width)

    def kernel(length_ref, query_ref, pair_ref, out_ref):
        bag, group = lax.axis_index("bag"), lax.axis_index("ulysses")
        chip, core = bag // CORES, bag % CORES

        def sequence_of(row, ends):
            owner = ((row // block) ^ chip) * CORES + (row // span_len % CORES ^ core)
            place = (row // (CORES * span_len) % group_count) ^ group
            position = (place * bag_count + owner) * span_len + row % span_len
            sequence = jnp.zeros(row.shape, jnp.int32)
            for end in ends:
                sequence = sequence + (position >= end).astype(jnp.int32)
            return sequence

        def rows(tile):
            return tile.astype(jnp.float32).reshape(-1, width).astype(jnp.bfloat16)

        masks, scores = [], []
        for at in range(chips):
            table = length_ref[at ^ chip].astype(jnp.float32).astype(jnp.int32)
            end, ends = jnp.zeros((1, 1), jnp.int32), []
            for entry in range(seq_bag):
                end = end + table[2 * entry : 2 * entry + 1, :1] * BASE + table[2 * entry + 1 : 2 * entry + 2, :1]
                ends.append(end)
            query_seq = sequence_of(lax.broadcasted_iota(jnp.int32, (block, 1), 0), ends)
            masks.append(query_seq == sequence_of(lax.broadcasted_iota(jnp.int32, (1, chips * block), 1), ends))
        units = [(at, head) for at in range(chips) for head in range(heads)]
        for at, head in units:
            score = lax.dot_general(
                rows(query_ref[:, :, at, head]),
                rows(pair_ref[:, 0, :, :, at, head]),
                (((1,), (1,)), ((), ())),
                preferred_element_type=jnp.float32,
            )
            scores.append(jnp.where(masks[at], score * scale, -jnp.inf))
        for (at, head), score in zip(units, scores):
            expo = jnp.exp(score - jnp.max(score, axis=-1, keepdims=True))
            weights = (expo * (1.0 / jnp.sum(expo, axis=-1, keepdims=True))).astype(jnp.bfloat16)
            output = jnp.dot(weights, rows(pair_ref[:, 1, :, :, at, head]), preferred_element_type=jnp.float32)
            out_ref[:, :, at, head] = output.reshape(group_count, CORES, span_len, width).astype(out_ref.dtype)

    return pl.pallas_call(
        kernel,
        out_shape=jax.ShapeDtypeStruct(queries.shape, queries.dtype),
        in_specs=[pl.BlockSpec(memory_space=pltpu.VMEM)] * 3,
        out_specs=pl.BlockSpec(memory_space=pltpu.VMEM),
        compiler_params=pltpu.CompilerParams(vmem_limit_bytes=8 << 20),
        cost_estimate=pl.CostEstimate(
            flops=4 * heads * chips * chips * block * block * width,
            bytes_accessed=keys_values.nbytes + 2 * queries.nbytes,
            transcendentals=heads * chips * chips * block * block,
        ),
        name="attend_plane",
    )(lengths, queries, keys_values)


def attend(lengths, packed, bag_count, group_count, after=()):
    slots, _, heads_here, span_len, width = packed.shape
    bag_tok = slots * span_len
    block = min(256, bag_tok)
    block_slots = block // span_len
    seq_bag = lengths.shape[1]
    scale = 1.0 / math.sqrt(width)

    def sequence_of(row, length_ref):
        slot, offset = row // span_len, row % span_len
        group, owner = slot // bag_count, slot % (bag_count // CORES) * CORES + slot % bag_count // (bag_count // CORES)
        position = (group * bag_count + owner) * span_len + offset
        end = jnp.zeros((1, 1), jnp.int32)
        sequence = jnp.zeros(row.shape, jnp.int32)
        for entry in range(seq_bag):
            end = end + length_ref[:, entry : entry + 1]
            sequence = sequence + (position >= end).astype(jnp.int32)
        return sequence

    def kernel(length_ref, packed_ref, *refs):
        out_ref = refs[-1]
        key_seq = sequence_of(lax.broadcasted_iota(jnp.int32, (1, bag_tok), 1), length_ref)

        def rows(kind, first, count, head):
            tile = packed_ref[pl.ds(first, count), kind, head]
            return tile.astype(jnp.float32).reshape(count * span_len, width).astype(jnp.bfloat16)

        def one_block(index, carry):
            first = index * block_slots
            row = index * block + lax.broadcasted_iota(jnp.int32, (block, 1), 0)
            same = sequence_of(row, length_ref) == key_seq
            scores = [
                lax.dot_general(
                    rows(0, first, block_slots, head),
                    rows(1, 0, slots, head),
                    (((1,), (1,)), ((), ())),
                    preferred_element_type=jnp.float32,
                )
                for head in range(heads_here)
            ]
            weights = []
            for score in scores:
                score = jnp.where(same, score * scale, -jnp.inf)
                expo = jnp.exp(score - jnp.max(score, axis=-1, keepdims=True))
                weights.append((expo * (1.0 / jnp.sum(expo, axis=-1, keepdims=True))).astype(jnp.bfloat16))
            for head in range(heads_here):
                output = jnp.dot(weights[head], rows(2, 0, slots, head), preferred_element_type=jnp.float32)
                output = output.reshape(block_slots, span_len, width).astype(out_ref.dtype)
                out_ref[pl.ds(first, block_slots), head] = output
            return carry

        if bag_tok == block:
            one_block(0, 0)
        else:
            lax.fori_loop(0, bag_tok // block, one_block, 0)

    return pl.pallas_call(
        kernel,
        out_shape=jax.ShapeDtypeStruct((slots, heads_here, span_len, width), packed.dtype),
        in_specs=[pl.BlockSpec(memory_space=pltpu.VMEM)] * 2 + [pl.BlockSpec(memory_space=pl.ANY)] * len(after),
        out_specs=pl.BlockSpec(memory_space=pltpu.VMEM),
        compiler_params=pltpu.CompilerParams(vmem_limit_bytes=32 << 20),
        name="attend_bag",
    )(lengths, packed, *after)


def exchange(rows):
    bag_count, group_count = lax.axis_size("bag"), lax.axis_size("ulysses")
    order = [
        bag * group_count + group
        for group in range(group_count)
        for core in range(CORES)
        for bag in range(core, bag_count, CORES)
    ]
    return lax.all_to_all(rows, AXES, split_axis=0, concat_axis=0, tiled=True, axis_index_groups=[order])


def shards(queries, keys, values, span_route, seq_lengths):
    bag_count = lax.axis_size("bag")
    group_count = lax.axis_size("ulysses")
    tok_dev, row_width = queries.shape
    span_len = tok_dev // bag_count
    heads_here = row_width // HDIM // group_count
    arrays = [
        rows.reshape(bag_count, span_len, group_count, heads_here, HDIM).transpose(0, 2, 3, 1, 4)
        for rows in (queries, keys, values)
    ]
    slots = (group_count, CORES, bag_count // CORES)
    powers = all(size & (size - 1) == 0 for size in (bag_count, group_count))
    if span_len >= 2 * seq_lengths.shape[1] and span_len % ROW_TILE == 0 and heads_here > SPREAD and bag_count > CORES and powers:
        packed, aside_q, aside_kv = pack_spans(span_route, seq_lengths, arrays, heads_here - SPREAD)
        across = swap(aside_kv, "bag", bag_count // 2)
        arrived = exchange(packed)
        blocks, tables = merge(aside_q, aside_kv, across)
        blocks = blocks.reshape(5, group_count, CORES, -1, SPREAD, span_len, HDIM)
        blocks = jnp.stack(swap_groups(swap_cores(blocks, 2).swapaxes(0, 1)), axis=1)
        pairs = blocks[1:].reshape(2, 2, *blocks.shape[1:])
        pairs, lengths = gather_chips(pairs, tables)
        settled = attend_plane(lengths, blocks[0], pairs, seq_lengths.shape[1], bag_count)
        settled = swap_cores(settled, 1)
        attended = attend(seq_lengths, arrived, bag_count, group_count, (blocks,))
        pieces = swap_groups(settled)
        returned = exchange(attended).reshape(*slots, *attended.shape[1:])
        result = unpack_spans(span_route, returned, pieces)
    else:
        route_mine = lax.dynamic_index_in_dim(span_route[0], lax.axis_index("ulysses"), 0, keepdims=False)
        packed = jnp.stack(arrays, axis=2)[jnp.argsort(route_mine)]
        packed = packed.reshape(*slots[:0:-1], *packed.shape[1:]).swapaxes(0, 2)
        packed = packed.reshape(bag_count * group_count, *packed.shape[3:])
        attended = attend(seq_lengths, exchange(packed), bag_count, group_count)
        returned = exchange(attended).reshape(*slots, *attended.shape[1:])
        result = returned.swapaxes(0, 2).reshape(bag_count, group_count, *attended.shape[1:])[route_mine]
    return result.transpose(0, 3, 1, 2, 4).reshape(tok_dev, row_width)


def solution(mesh):
    placed = (
        P(("bag", "ulysses"), None),
        P(("bag", "ulysses"), None),
        P(("bag", "ulysses"), None),
        P("bag", None, None),
        P("bag", None),
    )
    return jax.shard_map(
        shards, mesh=mesh, in_specs=placed, out_specs=P(("bag", "ulysses"), None), check_vma=False
    )
```

```python
import math

import jax
import jax.numpy as jnp
from jax import lax
from jax.experimental import pallas as pl
from jax.experimental.pallas import tpu as pltpu
from jax.sharding import PartitionSpec as P

HDIM = 128
ROW_TILE = 8
MARGIN = 1 << 20
SPREAD = 1
BASE = 128
PIECES = 4
CORES = 2
AXES = ("bag", "ulysses")


def pack_spans(span_route, seq_lengths, arrays, direct_heads):
    bag_count, group_count, heads_here, span_len, width = arrays[0].shape
    kinds, chips = len(arrays), bag_count // CORES
    spread = heads_here - direct_heads
    payload = sum(rows.nbytes for rows in arrays)

    seq_bag = seq_lengths.shape[1]
    each = bag_count * group_count * spread

    def kernel(route_hbm, lengths_hbm, *refs):
        sources, (target, aside_q, aside_kv), (stage, lengths, route_ref, sem) = refs[:kinds], refs[kinds : kinds + 3], refs[-4:]
        group, bag = lax.axis_index("ulysses"), lax.axis_index("bag")
        copies = [pltpu.make_async_copy(sources[k], stage.at[k], sem.at[k]) for k in range(kinds)]
        route_copy = pltpu.make_async_copy(route_hbm, route_ref, sem.at[kinds])
        route_copy.start()
        for copy in copies[1:] + copies[:1]:
            copy.start()
        lengths_copy = pltpu.make_async_copy(lengths_hbm, lengths, sem.at[kinds + 1])
        lengths_copy.start()
        route_copy.wait()
        lengths_copy.wait()
        row = lax.broadcasted_iota(jnp.int32, (span_len, width), 0)
        block = jnp.zeros((span_len, width), jnp.int32)
        for entry in range(seq_bag):
            length = lengths[:, entry : entry + 1]
            block = jnp.where(row == 2 * entry, length // BASE, jnp.where(row == 2 * entry + 1, length % BASE, block))
        aside_kv[(kinds - 1) * each] = block.astype(jnp.float32).astype(aside_kv.dtype)
        places = []
        for span in range(bag_count):
            to = route_ref[0, group, span]
            chip, core = lax.div(to, CORES), lax.rem(to, CORES)
            first = ((core ^ lax.rem(bag, CORES)) * chips + chip) * spread
            places.append((core, chip, [(other ^ group) * (CORES * chips * spread) + first for other in range(group_count)]))
        for kind in (*range(1, kinds), 0):
            copies[kind].wait()
            for span, (core, chip, blocks) in enumerate(places):
                target[:, core, chip, kind] = stage[kind, span, :, :direct_heads]
                for other in range(group_count):
                    for head in range(spread):
                        rows = stage[kind, span, other, direct_heads + head]
                        if kind == 0:
                            aside_q[blocks[other] + head] = rows
                        else:
                            aside_kv[(kind - 1) * each + blocks[other] + head] = rows

    shape = (group_count, CORES, bag_count // CORES, kinds, direct_heads, span_len, width)
    shape_aside = [(each, span_len, width), ((kinds - 1) * each + 1, span_len, width)]
    dtype = arrays[0].dtype
    packed, aside_q, aside_kv = pl.pallas_call(
        kernel,
        out_shape=[pltpu.VMEM(size, dtype) for size in (shape, *shape_aside)],
        in_specs=[pl.BlockSpec(memory_space=pl.ANY)] * (2 + kinds),
        out_specs=[pl.BlockSpec(memory_space=pltpu.VMEM)] * 3,
        scratch_shapes=[
            pltpu.VMEM((kinds, *arrays[0].shape), dtype),
            pltpu.VMEM(seq_lengths.shape, seq_lengths.dtype),
            pltpu.SMEM(span_route.shape, span_route.dtype),
            pltpu.SemaphoreType.DMA((kinds + 2,)),
        ],
        compiler_params=pltpu.CompilerParams(vmem_limit_bytes=2 * payload + MARGIN),
        name="pack_spans",
    )(*[pltpu.with_memory_space_constraint(rows, pltpu.HBM) for rows in (span_route, seq_lengths, *arrays)])
    return packed.reshape(bag_count * group_count, *shape[3:]), aside_q, aside_kv


def unpack_spans(span_route, returned, pieces):
    group_count, _, chips, direct_heads, span_len, width = returned.shape
    bag_count = chips * CORES
    spread = pieces[0].shape[2]

    def kernel(route_ref, source, *refs):
        aside, (target, span_of, sem) = refs[:-3], refs[-3:]
        group, bag = lax.axis_index("ulysses"), lax.axis_index("bag")
        for span in range(bag_count):
            at = route_ref[0, group, span]
            span_of[at] = span
            pltpu.make_async_copy(
                source.at[:, at % CORES, at // CORES], target.at[span, :, pl.ds(0, direct_heads)], sem
            ).start()
        for distance, piece in enumerate(aside):
            for core in range(CORES):
                for chip in range(chips):
                    pltpu.make_async_copy(
                        piece.at[core, chip],
                        target.at[span_of[chip * CORES + (bag % CORES ^ core)], group ^ distance, pl.ds(direct_heads, spread)],
                        sem,
                    ).start()
        pltpu.make_async_copy(target, target, sem).wait()

    shape = (bag_count, group_count, direct_heads + spread, span_len, width)
    return pl.pallas_call(
        kernel,
        out_shape=jax.ShapeDtypeStruct(shape, returned.dtype),
        in_specs=[pl.BlockSpec(memory_space=pltpu.VMEM)] * (2 + len(pieces)),
        out_specs=pl.BlockSpec(memory_space=pl.ANY),
        scratch_shapes=[pltpu.SMEM((bag_count,), jnp.int32), pltpu.SemaphoreType.DMA],
        compiler_params=pltpu.CompilerParams(vmem_limit_bytes=2 * returned.nbytes + MARGIN),
        name="unpack_spans",
    )(span_route, returned, *pieces)


def swap(rows, axis, distance):
    return lax.ppermute(rows, axis, [(index, index ^ distance) for index in range(lax.axis_size(axis))])


def swap_cores(rows, axis):
    kept, sent = (lax.index_in_dim(rows, core, axis, keepdims=False) for core in range(CORES))
    return jnp.stack([kept, swap(sent, "bag", 1)], axis=axis)


def swap_groups(rows):
    return [rows[0]] + [swap(rows[distance], "ulysses", distance) for distance in range(1, rows.shape[0])]


def settle(packed):
    slots = packed.shape[0]

    def kernel(source, target, sem):
        parts = [pl.ds(k * (slots // PIECES), slots // PIECES) for k in range(PIECES)]
        copies = [pltpu.make_async_copy(source.at[p], target.at[p], sem.at[k]) for k, p in enumerate(parts)]
        for copy in copies:
            copy.start()
        for copy in copies:
            copy.wait()

    return pl.pallas_call(
        kernel,
        out_shape=jax.ShapeDtypeStruct(packed.shape, packed.dtype),
        in_specs=[pl.BlockSpec(memory_space=pltpu.VMEM)],
        out_specs=pl.BlockSpec(memory_space=pl.ANY),
        scratch_shapes=[pltpu.SemaphoreType.DMA((PIECES,))],
        compiler_params=pltpu.CompilerParams(vmem_limit_bytes=2 * packed.nbytes + MARGIN),
        name="settle",
    )(packed)


def merge(queries, near, across):
    count, pair = queries.shape[0], near.shape[0] - 1
    size = queries.shape[1:]

    def kernel(query_ref, near_ref, across_ref, out_ref, length_ref):
        out_ref[:count] = query_ref[...]
        for index, ref in enumerate((near_ref, across_ref)):
            out_ref[count + index * pair : count + (index + 1) * pair] = ref[:pair]
            length_ref[index] = ref[pair]

    return pl.pallas_call(
        kernel,
        out_shape=[pltpu.VMEM((count + 2 * pair, *size), queries.dtype), pltpu.VMEM((2, *size), queries.dtype)],
        in_specs=[pl.BlockSpec(memory_space=pltpu.VMEM)] * 3,
        out_specs=[pl.BlockSpec(memory_space=pltpu.VMEM)] * 2,
        compiler_params=pltpu.CompilerParams(vmem_limit_bytes=4 << 20),
        cost_estimate=pl.CostEstimate(flops=1 << 35, bytes_accessed=1 << 26, transcendentals=0),
        name="merge",
    )(queries, near, across)


def gather_chips(near, lengths):
    chips = lax.axis_size("bag") // CORES
    size, distances = near.shape[1:], [0, chips // 2]
    step = chips // 4
    while step:
        count = near.shape[0]
        flat = jnp.concatenate([near.reshape(-1, *lengths.shape[1:]), lengths])
        flat = swap(flat, "bag", step * CORES)
        near = jnp.concatenate([near, flat[:-count].reshape(count, *size)])
        lengths = jnp.concatenate([lengths, flat[-count:]])
        distances, step = distances + [distance ^ step for distance in distances], step // 2
    order = [distances.index(distance) for distance in range(chips)]
    return jnp.stack([near[index] for index in order]), jnp.stack([lengths[index] for index in order])


def attend_plane(lengths, queries, keys_values, seq_bag, bag_count):
    group_count, _, chips, heads, span_len, width = queries.shape
    block = group_count * CORES * span_len
    scale = 1.0 / math.sqrt(width)

    def kernel(length_ref, query_ref, pair_ref, out_ref):
        bag, group = lax.axis_index("bag"), lax.axis_index("ulysses")
        chip, core = bag // CORES, bag % CORES

        def sequence_of(row, ends):
            owner = ((row // block) ^ chip) * CORES + (row // span_len % CORES ^ core)
            place = (row // (CORES * span_len) % group_count) ^ group
            position = (place * bag_count + owner) * span_len + row % span_len
            sequence = jnp.zeros(row.shape, jnp.int32)
            for end in ends:
                sequence = sequence + (position >= end).astype(jnp.int32)
            return sequence

        def rows(tile):
            return tile.astype(jnp.float32).reshape(-1, width).astype(jnp.bfloat16)

        masks, scores = [], []
        for at in range(chips):
            table = length_ref[at ^ chip].astype(jnp.float32).astype(jnp.int32)
            end, ends = jnp.zeros((1, 1), jnp.int32), []
            for entry in range(seq_bag):
                end = end + table[2 * entry : 2 * entry + 1, :1] * BASE + table[2 * entry + 1 : 2 * entry + 2, :1]
                ends.append(end)
            query_seq = sequence_of(lax.broadcasted_iota(jnp.int32, (block, 1), 0), ends)
            masks.append(query_seq == sequence_of(lax.broadcasted_iota(jnp.int32, (1, chips * block), 1), ends))
        units = [(at, head) for at in range(chips) for head in range(heads)]
        for at, head in units:
            score = lax.dot_general(
                rows(query_ref[:, :, at, head]),
                rows(pair_ref[:, 0, :, :, at, head]),
                (((1,), (1,)), ((), ())),
                preferred_element_type=jnp.float32,
            )
            scores.append(jnp.where(masks[at], score * scale, -jnp.inf))
        for (at, head), score in zip(units, scores):
            expo = jnp.exp(score - jnp.max(score, axis=-1, keepdims=True))
            weights = (expo * (1.0 / jnp.sum(expo, axis=-1, keepdims=True))).astype(jnp.bfloat16)
            output = jnp.dot(weights, rows(pair_ref[:, 1, :, :, at, head]), preferred_element_type=jnp.float32)
            out_ref[:, :, at, head] = output.reshape(group_count, CORES, span_len, width).astype(out_ref.dtype)

    return pl.pallas_call(
        kernel,
        out_shape=jax.ShapeDtypeStruct(queries.shape, queries.dtype),
        in_specs=[pl.BlockSpec(memory_space=pltpu.VMEM)] * 3,
        out_specs=pl.BlockSpec(memory_space=pltpu.VMEM),
        compiler_params=pltpu.CompilerParams(vmem_limit_bytes=8 << 20),
        cost_estimate=pl.CostEstimate(
            flops=4 * heads * chips * chips * block * block * width,
            bytes_accessed=keys_values.nbytes + 2 * queries.nbytes,
            transcendentals=heads * chips * chips * block * block,
        ),
        name="attend_plane",
    )(lengths, queries, keys_values)


def attend(lengths, packed, bag_count, group_count, after=()):
    slots, _, heads_here, span_len, width = packed.shape
    bag_tok = slots * span_len
    block = min(256, bag_tok)
    block_slots = block // span_len
    seq_bag = lengths.shape[1]
    scale = 1.0 / math.sqrt(width)

    def sequence_of(row, length_ref):
        slot, offset = row // span_len, row % span_len
        group, owner = slot // bag_count, slot % (bag_count // CORES) * CORES + slot % bag_count // (bag_count // CORES)
        position = (group * bag_count + owner) * span_len + offset
        end = jnp.zeros((1, 1), jnp.int32)
        sequence = jnp.zeros(row.shape, jnp.int32)
        for entry in range(seq_bag):
            end = end + length_ref[:, entry : entry + 1]
            sequence = sequence + (position >= end).astype(jnp.int32)
        return sequence

    def kernel(length_ref, packed_ref, *refs):
        out_ref = refs[-1]
        key_seq = sequence_of(lax.broadcasted_iota(jnp.int32, (1, bag_tok), 1), length_ref)

        def rows(kind, first, count, head):
            tile = packed_ref[pl.ds(first, count), kind, head]
            return tile.astype(jnp.float32).reshape(count * span_len, width).astype(jnp.bfloat16)

        def one_block(index, carry):
            first = index * block_slots
            row = index * block + lax.broadcasted_iota(jnp.int32, (block, 1), 0)
            same = sequence_of(row, length_ref) == key_seq
            scores = [
                lax.dot_general(
                    rows(0, first, block_slots, head),
                    rows(1, 0, slots, head),
                    (((1,), (1,)), ((), ())),
                    preferred_element_type=jnp.float32,
                )
                for head in range(heads_here)
            ]
            weights = []
            for score in scores:
                score = jnp.where(same, score * scale, -jnp.inf)
                expo = jnp.exp(score - jnp.max(score, axis=-1, keepdims=True))
                weights.append((expo * (1.0 / jnp.sum(expo, axis=-1, keepdims=True))).astype(jnp.bfloat16))
            for head in range(heads_here):
                output = jnp.dot(weights[head], rows(2, 0, slots, head), preferred_element_type=jnp.float32)
                output = output.reshape(block_slots, span_len, width).astype(out_ref.dtype)
                out_ref[pl.ds(first, block_slots), head] = output
            return carry

        if bag_tok == block:
            one_block(0, 0)
        else:
            lax.fori_loop(0, bag_tok // block, one_block, 0)

    return pl.pallas_call(
        kernel,
        out_shape=jax.ShapeDtypeStruct((slots, heads_here, span_len, width), packed.dtype),
        in_specs=[pl.BlockSpec(memory_space=pltpu.VMEM)] * 2 + [pl.BlockSpec(memory_space=pl.ANY)] * len(after),
        out_specs=pl.BlockSpec(memory_space=pltpu.VMEM),
        compiler_params=pltpu.CompilerParams(vmem_limit_bytes=32 << 20),
        name="attend_bag",
    )(lengths, packed, *after)


def exchange(rows):
    bag_count, group_count = lax.axis_size("bag"), lax.axis_size("ulysses")
    order = [
        bag * group_count + group
        for group in range(group_count)
        for core in range(CORES)
        for bag in range(core, bag_count, CORES)
    ]
    return lax.all_to_all(rows, AXES, split_axis=0, concat_axis=0, tiled=True, axis_index_groups=[order])


def shards(queries, keys, values, span_route, seq_lengths):
    bag_count = lax.axis_size("bag")
    group_count = lax.axis_size("ulysses")
    tok_dev, row_width = queries.shape
    span_len = tok_dev // bag_count
    heads_here = row_width // HDIM // group_count
    arrays = [
        rows.reshape(bag_count, span_len, group_count, heads_here, HDIM).transpose(0, 2, 3, 1, 4)
        for rows in (queries, keys, values)
    ]
    slots = (group_count, CORES, bag_count // CORES)
    powers = all(size & (size - 1) == 0 for size in (bag_count, group_count))
    if span_len >= 2 * seq_lengths.shape[1] and span_len % ROW_TILE == 0 and heads_here > SPREAD and bag_count > CORES and powers:
        packed, aside_q, aside_kv = pack_spans(span_route, seq_lengths, arrays, heads_here - SPREAD)
        across = swap(aside_kv, "bag", bag_count // 2)
        arrived = exchange(settle(packed))
        blocks, tables = merge(aside_q, aside_kv, across)
        blocks = blocks.reshape(5, group_count, CORES, -1, SPREAD, span_len, HDIM)
        blocks = jnp.stack(swap_groups(swap_cores(blocks, 2).swapaxes(0, 1)), axis=1)
        pairs = blocks[1:].reshape(2, 2, *blocks.shape[1:])
        pairs, lengths = gather_chips(pairs, tables)
        settled = attend_plane(lengths, blocks[0], pairs, seq_lengths.shape[1], bag_count)
        settled = swap_cores(settled, 1)
        attended = attend(seq_lengths, arrived, bag_count, group_count, (blocks,))
        pieces = swap_groups(settled)
        returned = exchange(attended).reshape(*slots, *attended.shape[1:])
        result = unpack_spans(span_route, returned, pieces)
    else:
        route_mine = lax.dynamic_index_in_dim(span_route[0], lax.axis_index("ulysses"), 0, keepdims=False)
        packed = jnp.stack(arrays, axis=2)[jnp.argsort(route_mine)]
        packed = packed.reshape(*slots[:0:-1], *packed.shape[1:]).swapaxes(0, 2)
        packed = packed.reshape(bag_count * group_count, *packed.shape[3:])
        attended = attend(seq_lengths, exchange(packed), bag_count, group_count)
        returned = exchange(attended).reshape(*slots, *attended.shape[1:])
        result = returned.swapaxes(0, 2).reshape(bag_count, group_count, *attended.shape[1:])[route_mine]
    return result.transpose(0, 3, 1, 2, 4).reshape(tok_dev, row_width)


def solution(mesh):
    placed = (
        P(("bag", "ulysses"), None),
        P(("bag", "ulysses"), None),
        P(("bag", "ulysses"), None),
        P("bag", None, None),
        P("bag", None),
    )
    return jax.shard_map(
        shards, mesh=mesh, in_specs=placed, out_specs=P(("bag", "ulysses"), None), check_vma=False
    )
```

```python
import math

import jax
import jax.numpy as jnp
from jax import lax
from jax.experimental import pallas as pl
from jax.experimental.pallas import tpu as pltpu
from jax.sharding import PartitionSpec as P

HDIM = 128
ROW_TILE = 8
MARGIN = 1 << 20
SPREAD = 1
BASE = 128
PIECES = 4
CORES = 2
PAIR = 1
AXES = ("bag", "ulysses")


def pack_spans(span_route, seq_lengths, arrays, direct_heads):
    bag_count, group_count, heads_here, span_len, width = arrays[0].shape
    kinds, chips = len(arrays), bag_count // CORES
    spread = heads_here - direct_heads
    payload = sum(rows.nbytes for rows in arrays)

    seq_bag = seq_lengths.shape[1]
    each = bag_count * group_count * spread

    def kernel(route_hbm, lengths_hbm, *refs):
        sources, (target, aside_q, aside_kv), (stage, lengths, route_ref, sem) = refs[:kinds], refs[kinds : kinds + 3], refs[-4:]
        group, bag = lax.axis_index("ulysses"), lax.axis_index("bag")
        copies = [pltpu.make_async_copy(sources[k], stage.at[k], sem.at[k]) for k in range(kinds)]
        route_copy = pltpu.make_async_copy(route_hbm, route_ref, sem.at[kinds])
        route_copy.start()
        for copy in copies[1:] + copies[:1]:
            copy.start()
        lengths_copy = pltpu.make_async_copy(lengths_hbm, lengths, sem.at[kinds + 1])
        lengths_copy.start()
        route_copy.wait()
        lengths_copy.wait()
        row = lax.broadcasted_iota(jnp.int32, (span_len, width), 0)
        block = jnp.zeros((span_len, width), jnp.int32)
        for entry in range(seq_bag):
            length = lengths[:, entry : entry + 1]
            block = jnp.where(row == 2 * entry, length // BASE, jnp.where(row == 2 * entry + 1, length % BASE, block))
        aside_kv[(kinds - 1) * each] = block.astype(jnp.float32).astype(aside_kv.dtype)
        places = []
        for span in range(bag_count):
            to = route_ref[0, group, span]
            chip, core = lax.div(to, CORES), lax.rem(to, CORES)
            first = ((core ^ lax.rem(bag, CORES)) * chips + chip) * spread
            places.append((core, chip, [(other ^ group) * (CORES * chips * spread) + first for other in range(group_count)]))
        for kind in (*range(1, kinds), 0):
            copies[kind].wait()
            for span, (core, chip, blocks) in enumerate(places):
                target[:, core, chip ^ PAIR, kind] = stage[kind, span, :, :direct_heads]
                for other in range(group_count):
                    for head in range(spread):
                        rows = stage[kind, span, other, direct_heads + head]
                        if kind == 0:
                            aside_q[blocks[other] + head] = rows
                        else:
                            aside_kv[(kind - 1) * each + blocks[other] + head] = rows

    shape = (group_count, CORES, bag_count // CORES, kinds, direct_heads, span_len, width)
    shape_aside = [(each, span_len, width), ((kinds - 1) * each + 1, span_len, width)]
    dtype = arrays[0].dtype
    packed, aside_q, aside_kv = pl.pallas_call(
        kernel,
        out_shape=[pltpu.VMEM(size, dtype) for size in (shape, *shape_aside)],
        in_specs=[pl.BlockSpec(memory_space=pl.ANY)] * (2 + kinds),
        out_specs=[pl.BlockSpec(memory_space=pltpu.VMEM)] * 3,
        scratch_shapes=[
            pltpu.VMEM((kinds, *arrays[0].shape), dtype),
            pltpu.VMEM(seq_lengths.shape, seq_lengths.dtype),
            pltpu.SMEM(span_route.shape, span_route.dtype),
            pltpu.SemaphoreType.DMA((kinds + 2,)),
        ],
        compiler_params=pltpu.CompilerParams(vmem_limit_bytes=2 * payload + MARGIN),
        name="pack_spans",
    )(*[pltpu.with_memory_space_constraint(rows, pltpu.HBM) for rows in (span_route, seq_lengths, *arrays)])
    return packed.reshape(bag_count * group_count, *shape[3:]), aside_q, aside_kv


def unpack_aside(span_route, shape, pieces):
    bag_count, group_count, heads_here = shape[:3]
    chips, spread = bag_count // CORES, pieces[0].shape[2]

    def kernel(route_ref, *refs):
        aside, (target, stage, sem) = refs[:-3], refs[-3:]
        group, bag = lax.axis_index("ulysses"), lax.axis_index("bag")
        part = pl.ds(heads_here - spread, spread)
        for span in range(bag_count):
            at = route_ref[0, group, span]
            chip, core = lax.div(at, CORES), lax.rem(at, CORES) ^ lax.rem(bag, CORES)
            for distance, piece in enumerate(aside):
                stage[span, group ^ distance] = piece[core, chip]
            pltpu.make_async_copy(stage.at[span], target.at[span, :, part], sem).start()
        pltpu.make_async_copy(stage, stage, sem).wait()

    return pl.pallas_call(
        kernel,
        out_shape=jax.ShapeDtypeStruct(shape, pieces[0].dtype),
        in_specs=[pl.BlockSpec(memory_space=pltpu.VMEM)] * (1 + len(pieces)),
        out_specs=pl.BlockSpec(memory_space=pl.ANY),
        scratch_shapes=[
            pltpu.VMEM((bag_count, group_count, spread, *shape[3:]), pieces[0].dtype),
            pltpu.SemaphoreType.DMA,
        ],
        compiler_params=pltpu.CompilerParams(vmem_limit_bytes=4 * MARGIN),
        name="unpack_aside",
    )(span_route, *pieces)


def unpack_spans(span_route, returned, output):
    group_count, _, chips, direct_heads = returned.shape[:4]
    bag_count = chips * CORES

    def kernel(route_ref, source, _, target, sem):
        group = lax.axis_index("ulysses")
        part = pl.ds(0, direct_heads)
        for span in range(bag_count):
            at = route_ref[0, group, span]
            pltpu.make_async_copy(source.at[:, at % CORES, (at // CORES) ^ PAIR], target.at[span, :, part], sem).start()
        pltpu.make_async_copy(source, source, sem).wait()

    return pl.pallas_call(
        kernel,
        out_shape=jax.ShapeDtypeStruct(output.shape, output.dtype),
        in_specs=[pl.BlockSpec(memory_space=pltpu.VMEM)] * 2 + [pl.BlockSpec(memory_space=pl.ANY)],
        out_specs=pl.BlockSpec(memory_space=pl.ANY),
        scratch_shapes=[pltpu.SemaphoreType.DMA],
        input_output_aliases={2: 0},
        compiler_params=pltpu.CompilerParams(vmem_limit_bytes=2 * returned.nbytes + MARGIN),
        name="unpack_spans",
    )(span_route, returned, output)


def swap(rows, axis, distance):
    return lax.ppermute(rows, axis, [(index, index ^ distance) for index in range(lax.axis_size(axis))])


def swap_cores(rows, axis):
    kept, sent = (lax.index_in_dim(rows, core, axis, keepdims=False) for core in range(CORES))
    return jnp.stack([kept, swap(sent, "bag", 1)], axis=axis)


def swap_groups(rows):
    return [rows[0]] + [swap(rows[distance], "ulysses", distance) for distance in range(1, rows.shape[0])]


def settle(packed):
    slots = packed.shape[0]

    def kernel(source, target, sem):
        parts = [pl.ds(k * (slots // PIECES), slots // PIECES) for k in range(PIECES)]
        copies = [pltpu.make_async_copy(source.at[p], target.at[p], sem.at[k]) for k, p in enumerate(parts)]
        for copy in copies:
            copy.start()
        for copy in copies:
            copy.wait()

    return pl.pallas_call(
        kernel,
        out_shape=jax.ShapeDtypeStruct(packed.shape, packed.dtype),
        in_specs=[pl.BlockSpec(memory_space=pltpu.VMEM)],
        out_specs=pl.BlockSpec(memory_space=pl.ANY),
        scratch_shapes=[pltpu.SemaphoreType.DMA((PIECES,))],
        compiler_params=pltpu.CompilerParams(vmem_limit_bytes=2 * packed.nbytes + MARGIN),
        name="settle",
    )(packed)


def merge(queries, near, across):
    count, pair = queries.shape[0], near.shape[0] - 1
    size = queries.shape[1:]

    def kernel(query_ref, near_ref, across_ref, out_ref, length_ref):
        out_ref[:count] = query_ref[...]
        for index, ref in enumerate((near_ref, across_ref)):
            out_ref[count + index * pair : count + (index + 1) * pair] = ref[:pair]
            length_ref[index] = ref[pair]

    return pl.pallas_call(
        kernel,
        out_shape=[pltpu.VMEM((count + 2 * pair, *size), queries.dtype), pltpu.VMEM((2, *size), queries.dtype)],
        in_specs=[pl.BlockSpec(memory_space=pltpu.VMEM)] * 3,
        out_specs=[pl.BlockSpec(memory_space=pltpu.VMEM)] * 2,
        compiler_params=pltpu.CompilerParams(vmem_limit_bytes=4 << 20),
        cost_estimate=pl.CostEstimate(flops=1 << 35, bytes_accessed=1 << 26, transcendentals=0),
        name="merge",
    )(queries, near, across)


def gather_chips(near, lengths):
    chips = lax.axis_size("bag") // CORES
    size, distances = near.shape[1:], [0, chips // 2]
    step = chips // 4
    while step:
        count = near.shape[0]
        flat = jnp.concatenate([near.reshape(-1, *lengths.shape[1:]), lengths])
        flat = swap(flat, "bag", step * CORES)
        near = jnp.concatenate([near, flat[:-count].reshape(count, *size)])
        lengths = jnp.concatenate([lengths, flat[-count:]])
        distances, step = distances + [distance ^ step for distance in distances], step // 2
    order = [distances.index(distance) for distance in range(chips)]
    return jnp.stack([near[index] for index in order]), jnp.stack([lengths[index] for index in order])


def attend_plane(lengths, queries, keys_values, seq_bag, bag_count):
    group_count, _, chips, heads, span_len, width = queries.shape
    block = group_count * CORES * span_len
    scale = 1.0 / math.sqrt(width)

    def kernel(length_ref, query_ref, pair_ref, out_ref):
        bag, group = lax.axis_index("bag"), lax.axis_index("ulysses")
        chip, core = bag // CORES, bag % CORES

        def sequence_of(row, ends):
            owner = ((row // block) ^ chip) * CORES + (row // span_len % CORES ^ core)
            place = (row // (CORES * span_len) % group_count) ^ group
            position = (place * bag_count + owner) * span_len + row % span_len
            sequence = jnp.zeros(row.shape, jnp.int32)
            for end in ends:
                sequence = sequence + (position >= end).astype(jnp.int32)
            return sequence

        def rows(tile):
            return tile.astype(jnp.float32).reshape(-1, width).astype(jnp.bfloat16)

        masks, scores = [], []
        for at in range(chips):
            table = length_ref[at ^ chip].astype(jnp.float32).astype(jnp.int32)
            end, ends = jnp.zeros((1, 1), jnp.int32), []
            for entry in range(seq_bag):
                end = end + table[2 * entry : 2 * entry + 1, :1] * BASE + table[2 * entry + 1 : 2 * entry + 2, :1]
                ends.append(end)
            query_seq = sequence_of(lax.broadcasted_iota(jnp.int32, (block, 1), 0), ends)
            masks.append(query_seq == sequence_of(lax.broadcasted_iota(jnp.int32, (1, chips * block), 1), ends))
        units = [(at, head) for at in range(chips) for head in range(heads)]
        for at, head in units:
            score = lax.dot_general(
                rows(query_ref[:, :, at, head]),
                rows(pair_ref[:, 0, :, :, at, head]),
                (((1,), (1,)), ((), ())),
                preferred_element_type=jnp.float32,
            )
            scores.append(jnp.where(masks[at], score * scale, -jnp.inf))
        for (at, head), score in zip(units, scores):
            expo = jnp.exp(score - jnp.max(score, axis=-1, keepdims=True))
            weights = (expo * (1.0 / jnp.sum(expo, axis=-1, keepdims=True))).astype(jnp.bfloat16)
            output = jnp.dot(weights, rows(pair_ref[:, 1, :, :, at, head]), preferred_element_type=jnp.float32)
            out_ref[:, :, at, head] = output.reshape(group_count, CORES, span_len, width).astype(out_ref.dtype)

    return pl.pallas_call(
        kernel,
        out_shape=jax.ShapeDtypeStruct(queries.shape, queries.dtype),
        in_specs=[pl.BlockSpec(memory_space=pltpu.VMEM)] * 3,
        out_specs=pl.BlockSpec(memory_space=pltpu.VMEM),
        compiler_params=pltpu.CompilerParams(vmem_limit_bytes=8 << 20),
        cost_estimate=pl.CostEstimate(
            flops=4 * heads * chips * chips * block * block * width,
            bytes_accessed=keys_values.nbytes + 2 * queries.nbytes,
            transcendentals=heads * chips * chips * block * block,
        ),
        name="attend_plane",
    )(lengths, queries, keys_values)


def attend(lengths, packed, bag_count, group_count, after=()):
    slots, _, heads_here, span_len, width = packed.shape
    bag_tok = slots * span_len
    block = min(256, bag_tok)
    block_slots = block // span_len
    seq_bag = lengths.shape[1]
    scale = 1.0 / math.sqrt(width)

    def sequence_of(row, length_ref):
        slot, offset = row // span_len, row % span_len
        group, owner = slot // bag_count, (slot % (bag_count // CORES) ^ PAIR) * CORES + slot % bag_count // (bag_count // CORES)
        position = (group * bag_count + owner) * span_len + offset
        end = jnp.zeros((1, 1), jnp.int32)
        sequence = jnp.zeros(row.shape, jnp.int32)
        for entry in range(seq_bag):
            end = end + length_ref[:, entry : entry + 1]
            sequence = sequence + (position >= end).astype(jnp.int32)
        return sequence

    def kernel(length_ref, packed_ref, *refs):
        out_ref = refs[-1]
        key_seq = sequence_of(lax.broadcasted_iota(jnp.int32, (1, bag_tok), 1), length_ref)

        def rows(kind, first, count, head):
            tile = packed_ref[pl.ds(first, count), kind, head]
            return tile.astype(jnp.float32).reshape(count * span_len, width).astype(jnp.bfloat16)

        def one_block(index, carry):
            first = index * block_slots
            row = index * block + lax.broadcasted_iota(jnp.int32, (block, 1), 0)
            same = sequence_of(row, length_ref) == key_seq
            scores = [
                lax.dot_general(
                    rows(0, first, block_slots, head),
                    rows(1, 0, slots, head),
                    (((1,), (1,)), ((), ())),
                    preferred_element_type=jnp.float32,
                )
                for head in range(heads_here)
            ]
            weights = []
            for score in scores:
                score = jnp.where(same, score * scale, -jnp.inf)
                expo = jnp.exp(score - jnp.max(score, axis=-1, keepdims=True))
                weights.append((expo * (1.0 / jnp.sum(expo, axis=-1, keepdims=True))).astype(jnp.bfloat16))
            for head in range(heads_here):
                output = jnp.dot(weights[head], rows(2, 0, slots, head), preferred_element_type=jnp.float32)
                output = output.reshape(block_slots, span_len, width).astype(out_ref.dtype)
                out_ref[pl.ds(first, block_slots), head] = output
            return carry

        if bag_tok == block:
            one_block(0, 0)
        else:
            lax.fori_loop(0, bag_tok // block, one_block, 0)

    return pl.pallas_call(
        kernel,
        out_shape=jax.ShapeDtypeStruct((slots, heads_here, span_len, width), packed.dtype),
        in_specs=[pl.BlockSpec(memory_space=pltpu.VMEM)] * 2 + [pl.BlockSpec(memory_space=pl.ANY)] * len(after),
        out_specs=pl.BlockSpec(memory_space=pltpu.VMEM),
        compiler_params=pltpu.CompilerParams(vmem_limit_bytes=32 << 20),
        name="attend_bag",
    )(lengths, packed, *after)


def exchange(rows):
    bag_count, group_count = lax.axis_size("bag"), lax.axis_size("ulysses")
    order = [
        bag * group_count + group
        for group in range(group_count)
        for core in range(CORES)
        for bag in [(chip ^ PAIR) * CORES + core for chip in range(bag_count // CORES)]
    ]
    return lax.all_to_all(rows, AXES, split_axis=0, concat_axis=0, tiled=True, axis_index_groups=[order])


def shards(queries, keys, values, span_route, seq_lengths):
    bag_count = lax.axis_size("bag")
    group_count = lax.axis_size("ulysses")
    tok_dev, row_width = queries.shape
    span_len = tok_dev // bag_count
    heads_here = row_width // HDIM // group_count
    arrays = [
        rows.reshape(bag_count, span_len, group_count, heads_here, HDIM).transpose(0, 2, 3, 1, 4)
        for rows in (queries, keys, values)
    ]
    slots = (group_count, CORES, bag_count // CORES)
    paired = jnp.array([chip ^ PAIR for chip in range(bag_count // CORES)])
    powers = all(size & (size - 1) == 0 for size in (bag_count, group_count))
    if span_len >= 2 * seq_lengths.shape[1] and span_len % ROW_TILE == 0 and heads_here > SPREAD and bag_count > CORES and powers:
        packed, aside_q, aside_kv = pack_spans(span_route, seq_lengths, arrays, heads_here - SPREAD)
        across = swap(aside_kv, "bag", bag_count // 2)
        arrived = exchange(settle(packed))
        blocks, tables = merge(aside_q, aside_kv, across)
        blocks = blocks.reshape(5, group_count, CORES, -1, SPREAD, span_len, HDIM)
        blocks = jnp.stack(swap_groups(swap_cores(blocks, 2).swapaxes(0, 1)), axis=1)
        pairs = blocks[1:].reshape(2, 2, *blocks.shape[1:])
        pairs, lengths = gather_chips(pairs, tables)
        settled = attend_plane(lengths, blocks[0], pairs, seq_lengths.shape[1], bag_count)
        settled = swap_cores(settled, 1)
        attended = attend(seq_lengths, arrived, bag_count, group_count, (blocks,))
        pieces = swap_groups(settled)
        returned = exchange(attended).reshape(*slots, *attended.shape[1:])
        output = unpack_aside(span_route, arrays[0].shape, pieces)
        result = unpack_spans(span_route, returned, output)
    else:
        route_mine = lax.dynamic_index_in_dim(span_route[0], lax.axis_index("ulysses"), 0, keepdims=False)
        packed = jnp.stack(arrays, axis=2)[jnp.argsort(route_mine)]
        packed = packed.reshape(*slots[:0:-1], *packed.shape[1:]).swapaxes(0, 2)[:, :, paired]
        packed = packed.reshape(bag_count * group_count, *packed.shape[3:])
        attended = attend(seq_lengths, exchange(packed), bag_count, group_count)
        returned = exchange(attended).reshape(*slots, *attended.shape[1:])[:, :, paired]
        result = returned.swapaxes(0, 2).reshape(bag_count, group_count, *attended.shape[1:])[route_mine]
    return result.transpose(0, 3, 1, 2, 4).reshape(tok_dev, row_width)


def solution(mesh):
    placed = (
        P(("bag", "ulysses"), None),
        P(("bag", "ulysses"), None),
        P(("bag", "ulysses"), None),
        P("bag", None, None),
        P("bag", None),
    )
    return jax.shard_map(
        shards, mesh=mesh, in_specs=placed, out_specs=P(("bag", "ulysses"), None), check_vma=False
    )
```

```python
import math

import jax
import jax.numpy as jnp
from jax import lax
from jax.experimental import pallas as pl
from jax.experimental.pallas import tpu as pltpu
from jax.sharding import PartitionSpec as P

HDIM = 128
ROW_TILE = 8
MARGIN = 1 << 20
SPREAD = 1
BASE = 128
PIECES = 4
CORES = 2
PAIR = 1
ROWS = 256
AXES = ("bag", "ulysses")


def pack_spans(span_route, seq_lengths, arrays, direct_heads):
    bag_count, group_count, heads_here, span_len, width = arrays[0].shape
    kinds, chips = len(arrays), bag_count // CORES
    spread = heads_here - direct_heads
    payload = sum(rows.nbytes for rows in arrays)

    seq_bag = seq_lengths.shape[1]
    each = bag_count * group_count * spread

    def kernel(route_hbm, lengths_hbm, *refs):
        sources, (target, aside_q, aside_kv), (stage, lengths, route_ref, sem) = refs[:kinds], refs[kinds : kinds + 3], refs[-4:]
        group, bag = lax.axis_index("ulysses"), lax.axis_index("bag")
        copies = [pltpu.make_async_copy(sources[k], stage.at[k], sem.at[k]) for k in range(kinds)]
        route_copy = pltpu.make_async_copy(route_hbm, route_ref, sem.at[kinds])
        route_copy.start()
        for copy in copies[1:] + copies[:1]:
            copy.start()
        lengths_copy = pltpu.make_async_copy(lengths_hbm, lengths, sem.at[kinds + 1])
        lengths_copy.start()
        route_copy.wait()
        lengths_copy.wait()
        row = lax.broadcasted_iota(jnp.int32, (span_len, width), 0)
        block = jnp.zeros((span_len, width), jnp.int32)
        for entry in range(seq_bag):
            length = lengths[:, entry : entry + 1]
            block = jnp.where(row == 2 * entry, length // BASE, jnp.where(row == 2 * entry + 1, length % BASE, block))
        aside_kv[(kinds - 1) * each] = block.astype(jnp.float32).astype(aside_kv.dtype)
        places = []
        for span in range(bag_count):
            to = route_ref[0, group, span]
            chip, core = lax.div(to, CORES), lax.rem(to, CORES)
            first = ((core ^ lax.rem(bag, CORES)) * chips + chip) * spread
            places.append((core, chip, [(other ^ group) * (CORES * chips * spread) + first for other in range(group_count)]))
        for kind in (*range(1, kinds), 0):
            copies[kind].wait()
            for span, (core, chip, blocks) in enumerate(places):
                target[:, core, chip ^ PAIR, kind] = stage[kind, span, :, :direct_heads]
                for other in range(group_count):
                    for head in range(spread):
                        rows = stage[kind, span, other, direct_heads + head]
                        if kind == 0:
                            aside_q[blocks[other] + head] = rows
                        else:
                            aside_kv[(kind - 1) * each + blocks[other] + head] = rows

    shape = (group_count, CORES, bag_count // CORES, kinds, direct_heads, span_len, width)
    shape_aside = [(each, span_len, width), ((kinds - 1) * each + 1, span_len, width)]
    dtype = arrays[0].dtype
    packed, aside_q, aside_kv = pl.pallas_call(
        kernel,
        out_shape=[pltpu.VMEM(size, dtype) for size in (shape, *shape_aside)],
        in_specs=[pl.BlockSpec(memory_space=pl.ANY)] * (2 + kinds),
        out_specs=[pl.BlockSpec(memory_space=pltpu.VMEM)] * 3,
        scratch_shapes=[
            pltpu.VMEM((kinds, *arrays[0].shape), dtype),
            pltpu.VMEM(seq_lengths.shape, seq_lengths.dtype),
            pltpu.SMEM(span_route.shape, span_route.dtype),
            pltpu.SemaphoreType.DMA((kinds + 2,)),
        ],
        compiler_params=pltpu.CompilerParams(vmem_limit_bytes=2 * payload + MARGIN),
        name="pack_spans",
    )(*[pltpu.with_memory_space_constraint(rows, pltpu.HBM) for rows in (span_route, seq_lengths, *arrays)])
    return packed.reshape(bag_count * group_count, *shape[3:]), aside_q, aside_kv


def unpack_aside(span_route, shape, pieces):
    bag_count, group_count, heads_here = shape[:3]
    chips, spread = bag_count // CORES, pieces[0].shape[2]

    def kernel(route_ref, *refs):
        aside, (target, stage, sem) = refs[:-3], refs[-3:]
        group, bag = lax.axis_index("ulysses"), lax.axis_index("bag")
        part = pl.ds(heads_here - spread, spread)
        for span in range(bag_count):
            at = route_ref[0, group, span]
            chip, core = lax.div(at, CORES), lax.rem(at, CORES) ^ lax.rem(bag, CORES)
            for distance, piece in enumerate(aside):
                stage[span, group ^ distance] = piece[core, chip]
            pltpu.make_async_copy(stage.at[span], target.at[span, :, part], sem).start()
        pltpu.make_async_copy(stage, stage, sem).wait()

    return pl.pallas_call(
        kernel,
        out_shape=jax.ShapeDtypeStruct(shape, pieces[0].dtype),
        in_specs=[pl.BlockSpec(memory_space=pltpu.VMEM)] * (1 + len(pieces)),
        out_specs=pl.BlockSpec(memory_space=pl.ANY),
        scratch_shapes=[
            pltpu.VMEM((bag_count, group_count, spread, *shape[3:]), pieces[0].dtype),
            pltpu.SemaphoreType.DMA,
        ],
        compiler_params=pltpu.CompilerParams(vmem_limit_bytes=4 * MARGIN),
        name="unpack_aside",
    )(span_route, *pieces)


def unpack_spans(span_route, returned, output):
    group_count, _, chips, direct_heads = returned.shape[:4]
    bag_count = chips * CORES

    def kernel(route_ref, source, _, target, sem):
        group = lax.axis_index("ulysses")
        part = pl.ds(0, direct_heads)
        for span in range(bag_count):
            at = route_ref[0, group, span]
            pltpu.make_async_copy(source.at[:, at % CORES, at // CORES], target.at[span, :, part], sem).start()
        pltpu.make_async_copy(source, source, sem).wait()

    return pl.pallas_call(
        kernel,
        out_shape=jax.ShapeDtypeStruct(output.shape, output.dtype),
        in_specs=[pl.BlockSpec(memory_space=pltpu.VMEM)] * 2 + [pl.BlockSpec(memory_space=pl.ANY)],
        out_specs=pl.BlockSpec(memory_space=pl.ANY),
        scratch_shapes=[pltpu.SemaphoreType.DMA],
        input_output_aliases={2: 0},
        compiler_params=pltpu.CompilerParams(vmem_limit_bytes=2 * returned.nbytes + MARGIN),
        name="unpack_spans",
    )(span_route, returned, output)


def swap(rows, axis, distance):
    return lax.ppermute(rows, axis, [(index, index ^ distance) for index in range(lax.axis_size(axis))])


def swap_cores(rows, axis):
    kept, sent = (lax.index_in_dim(rows, core, axis, keepdims=False) for core in range(CORES))
    return jnp.stack([kept, swap(sent, "bag", 1)], axis=axis)


def swap_groups(rows):
    return [rows[0]] + [swap(rows[distance], "ulysses", distance) for distance in range(1, rows.shape[0])]


def settle(packed):
    slots = packed.shape[0]

    def kernel(source, target, sem):
        parts = [pl.ds(k * (slots // PIECES), slots // PIECES) for k in range(PIECES)]
        copies = [pltpu.make_async_copy(source.at[p], target.at[p], sem.at[k]) for k, p in enumerate(parts)]
        for copy in copies:
            copy.start()
        for copy in copies:
            copy.wait()

    return pl.pallas_call(
        kernel,
        out_shape=jax.ShapeDtypeStruct(packed.shape, packed.dtype),
        in_specs=[pl.BlockSpec(memory_space=pltpu.VMEM)],
        out_specs=pl.BlockSpec(memory_space=pl.ANY),
        scratch_shapes=[pltpu.SemaphoreType.DMA((PIECES,))],
        compiler_params=pltpu.CompilerParams(vmem_limit_bytes=2 * packed.nbytes + MARGIN),
        name="settle",
    )(packed)


def merge(queries, near, across):
    count, pair = queries.shape[0], near.shape[0] - 1
    size = queries.shape[1:]

    def kernel(query_ref, near_ref, across_ref, out_ref, length_ref):
        out_ref[:count] = query_ref[...]
        for index, ref in enumerate((near_ref, across_ref)):
            out_ref[count + index * pair : count + (index + 1) * pair] = ref[:pair]
            length_ref[index] = ref[pair]

    return pl.pallas_call(
        kernel,
        out_shape=[pltpu.VMEM((count + 2 * pair, *size), queries.dtype), pltpu.VMEM((2, *size), queries.dtype)],
        in_specs=[pl.BlockSpec(memory_space=pltpu.VMEM)] * 3,
        out_specs=[pl.BlockSpec(memory_space=pltpu.VMEM)] * 2,
        compiler_params=pltpu.CompilerParams(vmem_limit_bytes=4 << 20),
        cost_estimate=pl.CostEstimate(flops=1 << 35, bytes_accessed=1 << 26, transcendentals=0),
        name="merge",
    )(queries, near, across)


def gather_chips(near, lengths):
    chips = lax.axis_size("bag") // CORES
    size, distances = near.shape[1:], [0, chips // 2]
    step = chips // 4
    while step:
        count = near.shape[0]
        flat = jnp.concatenate([near.reshape(-1, *lengths.shape[1:]), lengths])
        flat = swap(flat, "bag", step * CORES)
        near = jnp.concatenate([near, flat[:-count].reshape(count, *size)])
        lengths = jnp.concatenate([lengths, flat[-count:]])
        distances, step = distances + [distance ^ step for distance in distances], step // 2
    order = [distances.index(distance) for distance in range(chips)]
    return jnp.stack([near[index] for index in order]), jnp.stack([lengths[index] for index in order])


def attend_plane(lengths, queries, keys_values, seq_bag, bag_count):
    group_count, _, chips, heads, span_len, width = queries.shape
    block = group_count * CORES * span_len
    scale = 1.0 / math.sqrt(width)

    def kernel(length_ref, query_ref, pair_ref, out_ref):
        bag, group = lax.axis_index("bag"), lax.axis_index("ulysses")
        chip, core = bag // CORES, bag % CORES

        def sequence_of(row, ends):
            owner = ((row // block) ^ chip) * CORES + (row // span_len % CORES ^ core)
            place = (row // (CORES * span_len) % group_count) ^ group
            position = (place * bag_count + owner) * span_len + row % span_len
            sequence = jnp.zeros(row.shape, jnp.int32)
            for end in ends:
                sequence = sequence + (position >= end).astype(jnp.int32)
            return sequence

        def rows(tile):
            return tile.astype(jnp.float32).reshape(-1, width).astype(jnp.bfloat16)

        masks, scores = [], []
        for at in range(chips):
            table = length_ref[at ^ chip].astype(jnp.float32).astype(jnp.int32)
            end, ends = jnp.zeros((1, 1), jnp.int32), []
            for entry in range(seq_bag):
                end = end + table[2 * entry : 2 * entry + 1, :1] * BASE + table[2 * entry + 1 : 2 * entry + 2, :1]
                ends.append(end)
            query_seq = sequence_of(lax.broadcasted_iota(jnp.int32, (block, 1), 0), ends)
            masks.append(query_seq == sequence_of(lax.broadcasted_iota(jnp.int32, (1, chips * block), 1), ends))
        units = [(at, head) for at in range(chips) for head in range(heads)]
        for at, head in units:
            score = lax.dot_general(
                rows(query_ref[:, :, at, head]),
                rows(pair_ref[:, 0, :, :, at, head]),
                (((1,), (1,)), ((), ())),
                preferred_element_type=jnp.float32,
            )
            scores.append(jnp.where(masks[at], score * scale, -jnp.inf))
        for (at, head), score in zip(units, scores):
            expo = jnp.exp(score - jnp.max(score, axis=-1, keepdims=True))
            weights = (expo * (1.0 / jnp.sum(expo, axis=-1, keepdims=True))).astype(jnp.bfloat16)
            output = jnp.dot(weights, rows(pair_ref[:, 1, :, :, at, head]), preferred_element_type=jnp.float32)
            out_ref[:, :, at, head] = output.reshape(group_count, CORES, span_len, width).astype(out_ref.dtype)

    return pl.pallas_call(
        kernel,
        out_shape=jax.ShapeDtypeStruct(queries.shape, queries.dtype),
        in_specs=[pl.BlockSpec(memory_space=pltpu.VMEM)] * 3,
        out_specs=pl.BlockSpec(memory_space=pltpu.VMEM),
        compiler_params=pltpu.CompilerParams(vmem_limit_bytes=8 << 20),
        cost_estimate=pl.CostEstimate(
            flops=4 * heads * chips * chips * block * block * width,
            bytes_accessed=keys_values.nbytes + 2 * queries.nbytes,
            transcendentals=heads * chips * chips * block * block,
        ),
        name="attend_plane",
    )(lengths, queries, keys_values)


def attend(lengths, packed, bag_count, group_count, after=(), back=None):
    slots, _, heads_here, span_len, width = packed.shape
    bag_tok = slots * span_len
    block = min(ROWS, bag_tok)
    block_slots = block // span_len
    seq_bag = lengths.shape[1]
    scale = 1.0 / math.sqrt(width)

    def sequence_of(row, length_ref):
        slot, offset = row // span_len, row % span_len
        group, owner = slot // bag_count, (slot % (bag_count // CORES) ^ PAIR) * CORES + slot % bag_count // (bag_count // CORES)
        position = (group * bag_count + owner) * span_len + offset
        end = jnp.zeros((1, 1), jnp.int32)
        sequence = jnp.zeros(row.shape, jnp.int32)
        for entry in range(seq_bag):
            end = end + length_ref[:, entry : entry + 1]
            sequence = sequence + (position >= end).astype(jnp.int32)
        return sequence

    def kernel(length_ref, packed_ref, *refs):
        out_ref = refs[-1]
        key_seq = sequence_of(lax.broadcasted_iota(jnp.int32, (1, bag_tok), 1), length_ref)

        def rows(kind, first, count, head):
            tile = packed_ref[pl.ds(first, count), kind, head]
            return tile.astype(jnp.float32).reshape(count * span_len, width).astype(jnp.bfloat16)

        def one_block(index, carry):
            first = index * block_slots
            row = index * block + lax.broadcasted_iota(jnp.int32, (block, 1), 0)
            same = sequence_of(row, length_ref) == key_seq
            scores = [
                lax.dot_general(
                    rows(0, first, block_slots, head),
                    rows(1, 0, slots, head),
                    (((1,), (1,)), ((), ())),
                    preferred_element_type=jnp.float32,
                )
                for head in range(heads_here)
            ]
            weights = []
            for score in scores:
                score = jnp.where(same, score * scale, -jnp.inf)
                expo = jnp.exp(score - jnp.max(score, axis=-1, keepdims=True))
                weights.append((expo * (1.0 / jnp.sum(expo, axis=-1, keepdims=True))).astype(jnp.bfloat16))
            for head in range(heads_here):
                output = jnp.dot(weights[head], rows(2, 0, slots, head), preferred_element_type=jnp.float32)
                output = output.reshape(block_slots, span_len, width).astype(out_ref.dtype)
                if back:
                    output = output.reshape(group_count, CORES, len(back), span_len, width)
                    for slot, chip in enumerate(back):
                        out_ref[:, :, slot, head] = output[:, :, chip ^ PAIR]
                else:
                    out_ref[pl.ds(first, block_slots), head] = output
            return carry

        if bag_tok == block:
            one_block(0, 0)
        else:
            lax.fori_loop(0, bag_tok // block, one_block, 0)

    return pl.pallas_call(
        kernel,
        out_shape=jax.ShapeDtypeStruct(
            (*((group_count, CORES, len(back)) if back else (slots,)), heads_here, span_len, width), packed.dtype
        ),
        in_specs=[pl.BlockSpec(memory_space=pltpu.VMEM)] * 2 + [pl.BlockSpec(memory_space=pl.ANY)] * len(after),
        out_specs=pl.BlockSpec(memory_space=pltpu.VMEM),
        compiler_params=pltpu.CompilerParams(vmem_limit_bytes=32 << 20),
        name="attend_bag",
    )(lengths, packed, *after)


def exchange(rows, chips=None):
    bag_count, group_count = lax.axis_size("bag"), lax.axis_size("ulysses")
    order = [
        bag * group_count + group
        for group in range(group_count)
        for core in range(CORES)
        for bag in [chip * CORES + core for chip in chips or [k ^ PAIR for k in range(bag_count // CORES)]]
    ]
    return lax.all_to_all(rows, AXES, split_axis=0, concat_axis=0, tiled=True, axis_index_groups=[order])


def shards(queries, keys, values, span_route, seq_lengths):
    bag_count = lax.axis_size("bag")
    group_count = lax.axis_size("ulysses")
    tok_dev, row_width = queries.shape
    span_len = tok_dev // bag_count
    heads_here = row_width // HDIM // group_count
    arrays = [
        rows.reshape(bag_count, span_len, group_count, heads_here, HDIM).transpose(0, 2, 3, 1, 4)
        for rows in (queries, keys, values)
    ]
    slots = (group_count, CORES, bag_count // CORES)
    paired = jnp.array([chip ^ PAIR for chip in range(bag_count // CORES)])
    powers = all(size & (size - 1) == 0 for size in (bag_count, group_count))
    if span_len >= 2 * seq_lengths.shape[1] and span_len % ROW_TILE == 0 and bag_count * group_count * span_len <= ROWS and heads_here > SPREAD and bag_count > CORES and powers:
        packed, aside_q, aside_kv = pack_spans(span_route, seq_lengths, arrays, heads_here - SPREAD)
        across = swap(aside_kv, "bag", bag_count // 2)
        arrived = exchange(settle(packed))
        blocks, tables = merge(aside_q, aside_kv, across)
        blocks = blocks.reshape(5, group_count, CORES, -1, SPREAD, span_len, HDIM)
        blocks = jnp.stack(swap_groups(swap_cores(blocks, 2).swapaxes(0, 1)), axis=1)
        pairs = blocks[1:].reshape(2, 2, *blocks.shape[1:])
        pairs, lengths = gather_chips(pairs, tables)
        settled = attend_plane(lengths, blocks[0], pairs, seq_lengths.shape[1], bag_count)
        settled = swap_cores(settled, 1)
        back = list(range(bag_count // CORES))
        attended = attend(seq_lengths, arrived, bag_count, group_count, (blocks,), back)
        attended = attended.reshape(bag_count * group_count, *attended.shape[3:])
        pieces = swap_groups(settled)
        returned = exchange(attended, back).reshape(*slots, *attended.shape[1:])
        output = unpack_aside(span_route, arrays[0].shape, pieces)
        result = unpack_spans(span_route, returned, output)
    else:
        route_mine = lax.dynamic_index_in_dim(span_route[0], lax.axis_index("ulysses"), 0, keepdims=False)
        packed = jnp.stack(arrays, axis=2)[jnp.argsort(route_mine)]
        packed = packed.reshape(*slots[:0:-1], *packed.shape[1:]).swapaxes(0, 2)[:, :, paired]
        packed = packed.reshape(bag_count * group_count, *packed.shape[3:])
        attended = attend(seq_lengths, exchange(packed), bag_count, group_count)
        returned = exchange(attended).reshape(*slots, *attended.shape[1:])[:, :, paired]
        result = returned.swapaxes(0, 2).reshape(bag_count, group_count, *attended.shape[1:])[route_mine]
    return result.transpose(0, 3, 1, 2, 4).reshape(tok_dev, row_width)


def solution(mesh):
    placed = (
        P(("bag", "ulysses"), None),
        P(("bag", "ulysses"), None),
        P(("bag", "ulysses"), None),
        P("bag", None, None),
        P("bag", None),
    )
    return jax.shard_map(
        shards, mesh=mesh, in_specs=placed, out_specs=P(("bag", "ulysses"), None), check_vma=False
    )
```

```python
import math

import jax
import jax.numpy as jnp
from jax import lax
from jax.experimental import pallas as pl
from jax.experimental.pallas import tpu as pltpu
from jax.sharding import PartitionSpec as P

HDIM = 128
ROW_TILE = 8
MARGIN = 1 << 20
SPREAD = 1
BASE = 128
PIECES = 4
CORES = 2
PAIR = 1
ROWS = 256
AXES = ("bag", "ulysses")


def pack_spans(span_route, seq_lengths, arrays, direct_heads):
    bag_count, group_count, heads_here, span_len, width = arrays[0].shape
    kinds, chips = len(arrays), bag_count // CORES
    spread = heads_here - direct_heads
    payload = sum(rows.nbytes for rows in arrays)

    seq_bag = seq_lengths.shape[1]
    each = bag_count * group_count * spread

    def kernel(route_hbm, lengths_hbm, *refs):
        sources, (target, aside_q, aside_kv), (stage, lengths, route_ref, sem) = refs[:kinds], refs[kinds : kinds + 3], refs[-4:]
        group, bag = lax.axis_index("ulysses"), lax.axis_index("bag")
        copies = [pltpu.make_async_copy(sources[k], stage.at[k], sem.at[k]) for k in range(kinds)]
        route_copy = pltpu.make_async_copy(route_hbm, route_ref, sem.at[kinds])
        route_copy.start()
        for copy in copies[1:] + copies[:1]:
            copy.start()
        lengths_copy = pltpu.make_async_copy(lengths_hbm, lengths, sem.at[kinds + 1])
        lengths_copy.start()
        route_copy.wait()
        lengths_copy.wait()
        row = lax.broadcasted_iota(jnp.int32, (span_len, width), 0)
        block = jnp.zeros((span_len, width), jnp.int32)
        for entry in range(seq_bag):
            length = lengths[:, entry : entry + 1]
            block = jnp.where(row == 2 * entry, length // BASE, jnp.where(row == 2 * entry + 1, length % BASE, block))
        aside_kv[(kinds - 1) * each] = block.astype(jnp.float32).astype(aside_kv.dtype)
        places = []
        for span in range(bag_count):
            to = route_ref[0, group, span]
            chip, core = lax.div(to, CORES), lax.rem(to, CORES)
            first = ((core ^ lax.rem(bag, CORES)) * chips + chip) * spread
            places.append((core, chip, [(other ^ group) * (CORES * chips * spread) + first for other in range(group_count)]))
        for kind in (*range(1, kinds), 0):
            copies[kind].wait()
            for span, (core, chip, blocks) in enumerate(places):
                target[:, core, chip ^ PAIR, kind] = stage[kind, span, :, :direct_heads]
                for other in range(group_count):
                    for head in range(spread):
                        rows = stage[kind, span, other, direct_heads + head]
                        if kind == 0:
                            aside_q[blocks[other] + head] = rows
                        else:
                            aside_kv[(kind - 1) * each + blocks[other] + head] = rows

    shape = (group_count, CORES, bag_count // CORES, kinds, direct_heads, span_len, width)
    shape_aside = [(each, span_len, width), ((kinds - 1) * each + 1, span_len, width)]
    dtype = arrays[0].dtype
    packed, aside_q, aside_kv = pl.pallas_call(
        kernel,
        out_shape=[pltpu.VMEM(size, dtype) for size in (shape, *shape_aside)],
        in_specs=[pl.BlockSpec(memory_space=pl.ANY)] * (2 + kinds),
        out_specs=[pl.BlockSpec(memory_space=pltpu.VMEM)] * 3,
        scratch_shapes=[
            pltpu.VMEM((kinds, *arrays[0].shape), dtype),
            pltpu.VMEM(seq_lengths.shape, seq_lengths.dtype),
            pltpu.SMEM(span_route.shape, span_route.dtype),
            pltpu.SemaphoreType.DMA((kinds + 2,)),
        ],
        compiler_params=pltpu.CompilerParams(vmem_limit_bytes=2 * payload + MARGIN),
        name="pack_spans",
    )(*[pltpu.with_memory_space_constraint(rows, pltpu.HBM) for rows in (span_route, seq_lengths, *arrays)])
    return packed.reshape(bag_count * group_count, *shape[3:]), aside_q, aside_kv


def unpack_aside(span_route, shape, pieces):
    bag_count, group_count, heads_here = shape[:3]
    chips, spread = bag_count // CORES, pieces[0].shape[2]

    def kernel(route_ref, *refs):
        aside, (target, stage, sem) = refs[:-3], refs[-3:]
        group, bag = lax.axis_index("ulysses"), lax.axis_index("bag")
        part = pl.ds(heads_here - spread, spread)
        for span in range(bag_count):
            at = route_ref[0, group, span]
            chip, core = lax.div(at, CORES), lax.rem(at, CORES) ^ lax.rem(bag, CORES)
            for distance, piece in enumerate(aside):
                stage[span, group ^ distance] = piece[core, chip]
            pltpu.make_async_copy(stage.at[span], target.at[span, :, part], sem).start()
        pltpu.make_async_copy(stage, stage, sem).wait()

    return pl.pallas_call(
        kernel,
        out_shape=jax.ShapeDtypeStruct(shape, pieces[0].dtype),
        in_specs=[pl.BlockSpec(memory_space=pltpu.VMEM)] * (1 + len(pieces)),
        out_specs=pl.BlockSpec(memory_space=pl.ANY),
        scratch_shapes=[
            pltpu.VMEM((bag_count, group_count, spread, *shape[3:]), pieces[0].dtype),
            pltpu.SemaphoreType.DMA,
        ],
        compiler_params=pltpu.CompilerParams(vmem_limit_bytes=4 * MARGIN),
        name="unpack_aside",
    )(span_route, *pieces)


def unpack_spans(span_route, returned, output):
    group_count, _, chips, direct_heads = returned.shape[:4]
    bag_count = chips * CORES

    def kernel(route_ref, source, _, target, sem):
        group = lax.axis_index("ulysses")
        part = pl.ds(0, direct_heads)
        for span in range(bag_count):
            at = route_ref[0, group, span]
            pltpu.make_async_copy(
                source.at[:, lax.rem(at, CORES), lax.div(at, CORES)], target.at[span, :, part], sem
            ).start()
        pltpu.make_async_copy(source, source, sem).wait()

    return pl.pallas_call(
        kernel,
        out_shape=jax.ShapeDtypeStruct(output.shape, output.dtype),
        in_specs=[pl.BlockSpec(memory_space=pltpu.VMEM)] * 2 + [pl.BlockSpec(memory_space=pl.ANY)],
        out_specs=pl.BlockSpec(memory_space=pl.ANY),
        scratch_shapes=[pltpu.SemaphoreType.DMA],
        input_output_aliases={2: 0},
        compiler_params=pltpu.CompilerParams(vmem_limit_bytes=2 * returned.nbytes + MARGIN),
        name="unpack_spans",
    )(span_route, returned, output)


def swap(rows, axis, distance):
    return lax.ppermute(rows, axis, [(index, index ^ distance) for index in range(lax.axis_size(axis))])


def swap_cores(rows, axis):
    kept, sent = (lax.index_in_dim(rows, core, axis, keepdims=False) for core in range(CORES))
    return jnp.stack([kept, swap(sent, "bag", 1)], axis=axis)


def swap_groups(rows):
    return [rows[0]] + [swap(rows[distance], "ulysses", distance) for distance in range(1, rows.shape[0])]


def settle(packed):
    slots = packed.shape[0]

    def kernel(source, target, sem):
        parts = [pl.ds(k * (slots // PIECES), slots // PIECES) for k in range(PIECES)]
        copies = [pltpu.make_async_copy(source.at[p], target.at[p], sem.at[k]) for k, p in enumerate(parts)]
        for copy in copies:
            copy.start()
        for copy in copies:
            copy.wait()

    return pl.pallas_call(
        kernel,
        out_shape=jax.ShapeDtypeStruct(packed.shape, packed.dtype),
        in_specs=[pl.BlockSpec(memory_space=pltpu.VMEM)],
        out_specs=pl.BlockSpec(memory_space=pl.ANY),
        scratch_shapes=[pltpu.SemaphoreType.DMA((PIECES,))],
        compiler_params=pltpu.CompilerParams(vmem_limit_bytes=2 * packed.nbytes + MARGIN),
        name="settle",
    )(packed)


def merge(queries, near, across):
    count, pair = queries.shape[0], near.shape[0] - 1
    size = queries.shape[1:]

    def kernel(query_ref, near_ref, across_ref, out_ref, length_ref):
        out_ref[:count] = query_ref[...]
        for index, ref in enumerate((near_ref, across_ref)):
            out_ref[count + index * pair : count + (index + 1) * pair] = ref[:pair]
            length_ref[index] = ref[pair]

    return pl.pallas_call(
        kernel,
        out_shape=[pltpu.VMEM((count + 2 * pair, *size), queries.dtype), pltpu.VMEM((2, *size), queries.dtype)],
        in_specs=[pl.BlockSpec(memory_space=pltpu.VMEM)] * 3,
        out_specs=[pl.BlockSpec(memory_space=pltpu.VMEM)] * 2,
        compiler_params=pltpu.CompilerParams(vmem_limit_bytes=4 << 20),
        cost_estimate=pl.CostEstimate(flops=1 << 35, bytes_accessed=1 << 26, transcendentals=0),
        name="merge",
    )(queries, near, across)


def gather_chips(near, lengths):
    chips = lax.axis_size("bag") // CORES
    size, distances = near.shape[1:], [0, chips // 2]
    step = chips // 4
    while step:
        count = near.shape[0]
        flat = jnp.concatenate([near.reshape(-1, *lengths.shape[1:]), lengths])
        flat = swap(flat, "bag", step * CORES)
        near = jnp.concatenate([near, flat[:-count].reshape(count, *size)])
        lengths = jnp.concatenate([lengths, flat[-count:]])
        distances, step = distances + [distance ^ step for distance in distances], step // 2
    order = [distances.index(distance) for distance in range(chips)]
    return jnp.stack([near[index] for index in order]), jnp.stack([lengths[index] for index in order])


def attend_plane(lengths, queries, keys_values, seq_bag, bag_count):
    group_count, _, chips, heads, span_len, width = queries.shape
    block = group_count * CORES * span_len
    scale = 1.0 / math.sqrt(width)

    def kernel(length_ref, query_ref, pair_ref, out_ref):
        bag, group = lax.axis_index("bag"), lax.axis_index("ulysses")
        chip, core = bag // CORES, bag % CORES

        def sequence_of(row, ends):
            owner = ((row // block) ^ chip) * CORES + (row // span_len % CORES ^ core)
            place = (row // (CORES * span_len) % group_count) ^ group
            position = (place * bag_count + owner) * span_len + row % span_len
            sequence = jnp.zeros(row.shape, jnp.int32)
            for end in ends:
                sequence = sequence + (position >= end).astype(jnp.int32)
            return sequence

        def rows(tile):
            return tile.astype(jnp.float32).reshape(-1, width).astype(jnp.bfloat16)

        masks, scores = [], []
        for at in range(chips):
            table = length_ref[at ^ chip].astype(jnp.float32).astype(jnp.int32)
            end, ends = jnp.zeros((1, 1), jnp.int32), []
            for entry in range(seq_bag):
                end = end + table[2 * entry : 2 * entry + 1, :1] * BASE + table[2 * entry + 1 : 2 * entry + 2, :1]
                ends.append(end)
            query_seq = sequence_of(lax.broadcasted_iota(jnp.int32, (block, 1), 0), ends)
            masks.append(query_seq == sequence_of(lax.broadcasted_iota(jnp.int32, (1, chips * block), 1), ends))
        units = [(at, head) for at in range(chips) for head in range(heads)]
        for at, head in units:
            score = lax.dot_general(
                rows(query_ref[:, :, at, head]),
                rows(pair_ref[:, 0, :, :, at, head]),
                (((1,), (1,)), ((), ())),
                preferred_element_type=jnp.float32,
            )
            scores.append(jnp.where(masks[at], score * scale, -jnp.inf))
        for (at, head), score in zip(units, scores):
            expo = jnp.exp(score - jnp.max(score, axis=-1, keepdims=True))
            weights = (expo * (1.0 / jnp.sum(expo, axis=-1, keepdims=True))).astype(jnp.bfloat16)
            output = jnp.dot(weights, rows(pair_ref[:, 1, :, :, at, head]), preferred_element_type=jnp.float32)
            out_ref[:, :, at, head] = output.reshape(group_count, CORES, span_len, width).astype(out_ref.dtype)

    return pl.pallas_call(
        kernel,
        out_shape=jax.ShapeDtypeStruct(queries.shape, queries.dtype),
        in_specs=[pl.BlockSpec(memory_space=pltpu.VMEM)] * 3,
        out_specs=pl.BlockSpec(memory_space=pltpu.VMEM),
        compiler_params=pltpu.CompilerParams(vmem_limit_bytes=8 << 20),
        cost_estimate=pl.CostEstimate(
            flops=4 * heads * chips * chips * block * block * width,
            bytes_accessed=keys_values.nbytes + 2 * queries.nbytes,
            transcendentals=heads * chips * chips * block * block,
        ),
        name="attend_plane",
    )(lengths, queries, keys_values)


def attend(lengths, packed, bag_count, group_count, after=(), back=None):
    slots, _, heads_here, span_len, width = packed.shape
    bag_tok = slots * span_len
    block = min(ROWS, bag_tok)
    block_slots = block // span_len
    seq_bag = lengths.shape[1]
    scale = 1.0 / math.sqrt(width)

    def sequence_of(row, length_ref):
        slot, offset = row // span_len, row % span_len
        group, owner = slot // bag_count, (slot % (bag_count // CORES) ^ PAIR) * CORES + slot % bag_count // (bag_count // CORES)
        position = (group * bag_count + owner) * span_len + offset
        end = jnp.zeros((1, 1), jnp.int32)
        sequence = jnp.zeros(row.shape, jnp.int32)
        for entry in range(seq_bag):
            end = end + length_ref[:, entry : entry + 1]
            sequence = sequence + (position >= end).astype(jnp.int32)
        return sequence

    def kernel(length_ref, packed_ref, *refs):
        out_ref = refs[-1]
        key_seq = sequence_of(lax.broadcasted_iota(jnp.int32, (1, bag_tok), 1), length_ref)

        def rows(kind, first, count, head):
            tile = packed_ref[pl.ds(first, count), kind, head]
            return tile.astype(jnp.float32).reshape(count * span_len, width).astype(jnp.bfloat16)

        def one_block(index, carry):
            first = index * block_slots
            row = index * block + lax.broadcasted_iota(jnp.int32, (block, 1), 0)
            same = sequence_of(row, length_ref) == key_seq
            scores = [
                lax.dot_general(
                    rows(0, first, block_slots, head),
                    rows(1, 0, slots, head),
                    (((1,), (1,)), ((), ())),
                    preferred_element_type=jnp.float32,
                )
                for head in range(heads_here)
            ]
            weights = []
            for score in scores:
                score = jnp.where(same, score * scale, -jnp.inf)
                expo = jnp.exp(score - jnp.max(score, axis=-1, keepdims=True))
                weights.append((expo * (1.0 / jnp.sum(expo, axis=-1, keepdims=True))).astype(jnp.bfloat16))
            for head in range(heads_here):
                output = jnp.dot(weights[head], rows(2, 0, slots, head), preferred_element_type=jnp.float32)
                output = output.reshape(block_slots, span_len, width).astype(out_ref.dtype)
                if back:
                    output = output.reshape(group_count, CORES, len(back), span_len, width)
                    for slot, chip in enumerate(back):
                        out_ref[:, :, slot, head] = output[:, :, chip ^ PAIR]
                else:
                    out_ref[pl.ds(first, block_slots), head] = output
            return carry

        if bag_tok == block:
            one_block(0, 0)
        else:
            lax.fori_loop(0, bag_tok // block, one_block, 0)

    return pl.pallas_call(
        kernel,
        out_shape=jax.ShapeDtypeStruct(
            (*((group_count, CORES, len(back)) if back else (slots,)), heads_here, span_len, width), packed.dtype
        ),
        in_specs=[pl.BlockSpec(memory_space=pltpu.VMEM)] * 2 + [pl.BlockSpec(memory_space=pl.ANY)] * len(after),
        out_specs=pl.BlockSpec(memory_space=pltpu.VMEM),
        compiler_params=pltpu.CompilerParams(vmem_limit_bytes=32 << 20),
        name="attend_bag",
    )(lengths, packed, *after)


def exchange(rows, chips=None):
    bag_count, group_count = lax.axis_size("bag"), lax.axis_size("ulysses")
    order = [
        bag * group_count + group
        for group in range(group_count)
        for core in range(CORES)
        for bag in [chip * CORES + core for chip in chips or [k ^ PAIR for k in range(bag_count // CORES)]]
    ]
    return lax.all_to_all(rows, AXES, split_axis=0, concat_axis=0, tiled=True, axis_index_groups=[order])


def shards(queries, keys, values, span_route, seq_lengths):
    bag_count = lax.axis_size("bag")
    group_count = lax.axis_size("ulysses")
    tok_dev, row_width = queries.shape
    span_len = tok_dev // bag_count
    heads_here = row_width // HDIM // group_count
    arrays = [
        rows.reshape(bag_count, span_len, group_count, heads_here, HDIM).transpose(0, 2, 3, 1, 4)
        for rows in (queries, keys, values)
    ]
    slots = (group_count, CORES, bag_count // CORES)
    paired = jnp.array([chip ^ PAIR for chip in range(bag_count // CORES)])
    powers = all(size & (size - 1) == 0 for size in (bag_count, group_count))
    if span_len >= 2 * seq_lengths.shape[1] and span_len % ROW_TILE == 0 and bag_count * group_count * span_len <= ROWS and heads_here > SPREAD and bag_count > CORES and powers:
        packed, aside_q, aside_kv = pack_spans(span_route, seq_lengths, arrays, heads_here - SPREAD)
        across = swap(aside_kv, "bag", bag_count // 2)
        arrived = exchange(settle(packed))
        blocks, tables = merge(aside_q, aside_kv, across)
        blocks = blocks.reshape(5, group_count, CORES, -1, SPREAD, span_len, HDIM)
        blocks = jnp.stack(swap_groups(swap_cores(blocks, 2).swapaxes(0, 1)), axis=1)
        pairs = blocks[1:].reshape(2, 2, *blocks.shape[1:])
        pairs, lengths = gather_chips(pairs, tables)
        settled = attend_plane(lengths, blocks[0], pairs, seq_lengths.shape[1], bag_count)
        settled = swap_cores(settled, 1)
        back = list(range(bag_count // CORES))
        attended = attend(seq_lengths, arrived, bag_count, group_count, (blocks,), back)
        attended = attended.reshape(bag_count * group_count, *attended.shape[3:])
        pieces = swap_groups(settled)
        returned = exchange(attended, back).reshape(*slots, *attended.shape[1:])
        output = unpack_aside(span_route, arrays[0].shape, pieces)
        result = unpack_spans(span_route, returned, output)
    else:
        route_mine = lax.dynamic_index_in_dim(span_route[0], lax.axis_index("ulysses"), 0, keepdims=False)
        packed = jnp.stack(arrays, axis=2)[jnp.argsort(route_mine)]
        packed = packed.reshape(*slots[:0:-1], *packed.shape[1:]).swapaxes(0, 2)[:, :, paired]
        packed = packed.reshape(bag_count * group_count, *packed.shape[3:])
        attended = attend(seq_lengths, exchange(packed), bag_count, group_count)
        returned = exchange(attended).reshape(*slots, *attended.shape[1:])[:, :, paired]
        result = returned.swapaxes(0, 2).reshape(bag_count, group_count, *attended.shape[1:])[route_mine]
    return result.transpose(0, 3, 1, 2, 4).reshape(tok_dev, row_width)


def solution(mesh):
    placed = (
        P(("bag", "ulysses"), None),
        P(("bag", "ulysses"), None),
        P(("bag", "ulysses"), None),
        P("bag", None, None),
        P("bag", None),
    )
    return jax.shard_map(
        shards, mesh=mesh, in_specs=placed, out_specs=P(("bag", "ulysses"), None), check_vma=False
    )
```
